128 devices in a mesh: tm: 16 (over y_hi, z, core), mesh: 8 (over x, y_lo).
Axes of the slice: x: 4, y: 4 (y_hi: 2, y_lo: 2; y = y_hi * 2 + y_lo), z: 4, core: 2. Of those that a mesh axis runs over, the one named last changes fastest.
Arguments:
- noise_slab: float32 [128, 262144], P('tm', 'mesh'), may hold values from -6 to 6
- lag_coef: float32 [8, 262144], P(None, 'mesh'), may hold values from -2.4 to 2.4
- precision_blocks: bfloat16 [4096, 4, 64, 64], P('mesh'), may hold values from -0.375 to 0.375
- block_cols: int32 [4096, 4], P('mesh'), may hold values from 0 to 4095, as said below
Outputs:
- sample_field: float32 [128, 262144], P('tm', 'mesh')
The draws below stay inside these ranges and needn't reach their ends.
Inputs may be any that keep to these rules, and one draw needn't show every extreme that they name: block_cols[b, 0] = b. The other entries of row b name blocks of the partition of b (blocks p * 512 to (p+1) * 512 - 1), except entry 1 of the first 16 blocks of a partition other than the first, which names one of the last 16 blocks of the partition before, and entry 1 of the last 16 blocks of a partition other than the last, which names one of the first 16 blocks of the partition after.
All inputs are finite; a program needn't handle non-finite values.
Results may differ from the reference program's by a relative error of at most 0.0033.
Values may be sent and summed in bfloat16 or wider, within the bound.
No kernel may reach another device: no remote copies, remote signals or barrier semaphores. Data moves between devices by JAX's collectives and lax.ppermute only.
A program may use at most 192 MiB of HBM per device.

```python
import jax
import jax.numpy as jnp
from jax import lax

BS = 64
K = 4
LAGS = 8
HB = 16
TD = 8
NB_DEV = 512
T_SIZE = 128
NBLK = 4096
NODES = 262144


def draw_block_cols(key, part):
    key = jax.random.fold_in(key, 11)
    row_ids = jnp.arange(NBLK, dtype=jnp.int32)
    owner = row_ids // NB_DEV
    position = row_ids % NB_DEV
    parts_count = NBLK // NB_DEV
    random_cols = jax.random.randint(key, (NBLK, K), 0, NB_DEV, dtype=jnp.int32) + owner[:, None] * NB_DEV
    lower = (position < HB) & (owner > 0)
    upper = (position >= NB_DEV - HB) & (owner < parts_count - 1)
    from_below = (owner - 1) * NB_DEV + NB_DEV - HB + position
    from_above = (owner + 1) * NB_DEV + position - (NB_DEV - HB)
    crossing = jnp.where(lower, from_below, jnp.where(upper, from_above, random_cols[:, 1]))
    result = random_cols.at[:, 0].set(row_ids).at[:, 1].set(crossing)
    return result.astype(jnp.int32)


def block_levels(own_key, extent, split, low, top_value):
    def one(dim, shards_of):
        draws = jax.random.uniform(jax.random.fold_in(jax.random.fold_in(own_key, 6), dim), (shards_of,), jnp.float32, low / len(split), top_value / len(split))
        return jnp.repeat(jnp.exp(draws), extent[dim] // shards_of).reshape((-1,) + (1,) * (len(extent) - dim - 1))

    level = one(*split[0])
    for cut in split[1:]:
        level = level * one(*cut)
    return level


def bell_draw(rng, shape, scale, bound, cuts=(), held_as=jnp.bfloat16):
    drawn = scale * jax.random.normal(rng, shape, jnp.float32)
    if cuts:
        drawn = drawn * block_levels(rng, shape, cuts, -0.22, 0.18)
    return jnp.clip(drawn, -bound, bound).astype(held_as)


def setup_inputs(seed: int = 0) -> dict:
    splits = jax.random.split(jax.random.key(seed), 5)
    return {
        "noise_slab": bell_draw(splits[0], (T_SIZE, NODES), 1.0, 6.0, ((0, 16), (1, 8)), jnp.float32),
        "lag_coef": bell_draw(splits[1], (LAGS, NODES), 0.4, 2.4, ((1, 8),), jnp.float32),
        "precision_blocks": bell_draw(splits[2], (NBLK, K, BS, BS), (BS * K) ** -0.5, 0.375, ((0, 8),)),
        "block_cols": draw_block_cols(jax.random.fold_in(splits[4], 71), 0),
    }


def apply_precision(field, precision_blocks, block_cols):
    field_half = field.astype(jnp.bfloat16)
    pieces = field_half.reshape(T_SIZE // TD, TD, NBLK, BS)
    weights = precision_blocks.astype(jnp.float32)

    def one_block(part):
        gathered = jnp.take(part, block_cols, axis=1).astype(jnp.float32)
        return jnp.einsum("rbkj,bkij->rbi", gathered, weights)

    result = lax.map(one_block, pieces)
    return result.reshape(T_SIZE, NODES)


def reference(noise_slab, lag_coef, precision_blocks, block_cols):
    mixed = jnp.zeros((T_SIZE, NODES), jnp.float32)
    for lag_index in range(LAGS):
        mixed = mixed + lag_coef[lag_index][None, :] * jnp.roll(noise_slab, lag_index, axis=0)
    cheb_one = apply_precision(mixed, precision_blocks, block_cols)
    cheb_two = 2.0 * apply_precision(cheb_one, precision_blocks, block_cols) - mixed
    cheb_three = 2.0 * apply_precision(cheb_two, precision_blocks, block_cols) - cheb_one
    filtered = 1.0 * mixed + 0.5 * cheb_one + 0.25 * cheb_two + 0.125 * cheb_three
    sample_field = jnp.zeros((T_SIZE, NODES), jnp.float32)
    for lag_index in range(LAGS):
        sample_field = sample_field + lag_coef[lag_index][None, :] * jnp.roll(filtered, -lag_index, axis=0)
    return sample_field
```

```python
import functools

import jax
import jax.numpy as jnp
from jax import lax
from jax.experimental import pallas as pl
from jax.experimental.pallas import tpu as pltpu
from jax.sharding import PartitionSpec as P

LANES = 128
HALF = 64
EDGE = 16
F32 = jnp.float32
BF16 = jnp.bfloat16
VSPEC = pl.BlockSpec(memory_space=pltpu.VMEM)
SSPEC = pl.BlockSpec(memory_space=pltpu.SMEM)
ASPEC = pl.BlockSpec(memory_space=pl.ANY)


def in_vmem(x):
    return pltpu.with_memory_space_constraint(x, pltpu.VMEM)


def lane_bits(rows):
    return lax.broadcasted_iota(jnp.int32, (rows, LANES), 1)


def repack_kernel(src, out, held, stage, sems):
    ks, width, depth, blocks = src.shape
    deep = depth // 16
    halves = blocks // (2 * LANES)
    units = ks * deep * halves

    def place(u):
        h = lax.rem(u, halves)
        rest = lax.div(u, halves)
        return lax.div(rest, deep), lax.rem(rest, deep), h

    def fetch(u, slot):
        k, jt, h = place(u)
        return pltpu.make_async_copy(
            src.at[k, :, pl.ds(pl.multiple_of(jt * 16, 16), 16), pl.ds(pl.multiple_of(h * 256, 256), 256)],
            held.at[slot],
            sems.at[slot],
        )

    lane = lane_bits(16)
    masks = [(lane & (1 << s)) != 0 for s in range(7)]

    fetch(0, 0).start()

    def unit(u, carry):
        slot = lax.rem(u, 2)

        @pl.when(u + 1 < units)
        def _():
            fetch(u + 1, 1 - slot).start()

        fetch(u, slot).wait()
        k, jt, h = place(u)
        row = pl.multiple_of(k * depth + jt * 16, 16)
        for r in range(8):
            vals = []
            for q in range(16):
                n = r + 8 * q
                v = held[slot, n % 64, :, LANES * (n // 64) : LANES * (n // 64) + LANES]
                vals.append(pltpu.roll(v, n, 1) if n else v)
            for s in range(4):
                vals = [jnp.where(masks[3 + s], vals[(q + (1 << s)) % 16], vals[q]) for q in range(16)]
            for q in range(16):
                stage[r + 8 * q] = vals[q]
        for c in range(8):
            vals = [stage[(16 * c + q) % 128] for q in range(23)]
            vals = [jnp.where(masks[2], vals[q + 4], vals[q]) for q in range(19)]
            vals = [jnp.where(masks[1], vals[q + 2], vals[q]) for q in range(17)]
            vals = [jnp.where(masks[0], vals[q + 1], vals[q]) for q in range(16)]
            for q in range(16):
                n = 16 * c + q
                m = (128 - n) % 128
                out[h, m, pl.ds(row, 16), :] = pltpu.roll(vals[q], n, 1) if n else vals[q]
        return carry

    lax.fori_loop(0, units, unit, 0)


def repack(blocks):
    src = jnp.transpose(blocks, (1, 2, 3, 0))
    ks, width, depth, count = src.shape
    return pl.pallas_call(
        repack_kernel,
        out_shape=pltpu.VMEM((count // 256, LANES, ks * depth, LANES), BF16),
        in_specs=[ASPEC],
        out_specs=VSPEC,
        scratch_shapes=[
            pltpu.VMEM((2, width, 16, 256), BF16),
            pltpu.VMEM((LANES, 16, LANES), BF16),
            pltpu.SemaphoreType.DMA((2,)),
        ],
        compiler_params=pltpu.CompilerParams(vmem_limit_bytes=8 << 20),
        cost_estimate=pl.CostEstimate(flops=0, bytes_accessed=40 << 20, transcendentals=0),
        name="repack",
    )(src)


def swap_pair(low, first, second):
    return (
        jnp.where(low, first, pltpu.roll(second, HALF, 1)),
        jnp.where(low, pltpu.roll(first, HALF, 1), second),
    )


def doubled(low, tile):
    turned = pltpu.roll(tile, HALF, 1)
    return jnp.where(low, tile, turned).astype(BF16), jnp.where(low, turned, tile).astype(BF16)


def mix_kernel(noise, prev, following, lag, mixed, half, lo, hi, ext):
    lags = lag.shape[0]
    steps = noise.shape[0]
    low = lane_bits(2 * steps) < HALF

    def tile(t, slot):
        cols = pl.ds(pl.multiple_of(t * LANES, LANES), LANES)
        ext[slot, 0:8, :] = prev[:, cols].astype(F32)
        ext[slot, 8:16, :] = noise[:, cols]
        ext[slot, 16:24, :] = following[:, cols].astype(F32)
        total = lag[0:1, cols] * ext[slot, 8:24, :]
        for l in range(1, lags):
            total = total + lag[l : l + 1, cols] * ext[slot, 8 - l : 24 - l, :]
        return total

    def step(i, carry):
        for j in range(4):
            g = i * 4 + j
            h = lax.div(g, 64)
            m = 2 * lax.rem(g, 64)
            t = h * 128 + lax.rem(g, 64)
            first = tile(t, 2 * j)
            second = tile(t + 64, 2 * j + 1)
            b = h * 256 + m
            half[b], half[b + 1] = doubled(low, first)
            half[b + 128], half[b + 129] = doubled(low, second)
            p = h * 128 + m
            mixed[p], mixed[p + 1] = swap_pair(low, first, second)
        return carry

    lax.fori_loop(0, 32, step, 0)
    lo[...] = half[0:EDGE]
    hi[...] = half[512 - EDGE : 512]


def mix(noise, prev, following, lag):
    rows = 2 * noise.shape[0]
    tiles = noise.shape[1] // LANES
    return pl.pallas_call(
        mix_kernel,
        out_shape=(
            pltpu.VMEM((tiles, rows, LANES), F32),
            pltpu.VMEM((2 * tiles, rows, LANES), BF16),
            jax.ShapeDtypeStruct((EDGE, rows, LANES), BF16),
            jax.ShapeDtypeStruct((EDGE, rows, LANES), BF16),
        ),
        in_specs=[VSPEC] * 4,
        out_specs=(VSPEC,) * 4,
        scratch_shapes=[pltpu.VMEM((8, 24, LANES), F32)],
        compiler_params=pltpu.CompilerParams(vmem_limit_bytes=8 << 20),
        cost_estimate=pl.CostEstimate(flops=8 << 20, bytes_accessed=8 << 20, transcendentals=0),
        name="mix",
    )(noise, prev, following, lag)


def group_product(g, cols, weights, half, low, below=None, above=None):
    h = lax.div(g, 64)
    m = 2 * lax.rem(g, 64)
    rows = []
    for j in range(4):
        b = h * 256 + (j % 2) * 128 + m + j // 2
        picked = []
        for k in range(4):
            c = cols[k, b]
            if below is None or k != 1:
                picked.append(half[c])
            else:
                own = half[jnp.clip(c, 0, 511)]
                under = below[jnp.clip(c + EDGE, 0, EDGE - 1)]
                over = above[jnp.clip(c - 512, 0, EDGE - 1)]
                picked.append(jnp.where(c < 0, under, jnp.where(c >= 512, over, own)))
        left = jnp.where(low, picked[0], picked[1])
        right = jnp.where(low, picked[2], picked[3])
        rows.append(jnp.concatenate([left, right], axis=1))
    taken = jnp.concatenate(rows, axis=0)
    tile = jnp.concatenate([weights[h, m], weights[h, m + 1]], axis=1)
    y = jnp.dot(taken, tile, preferred_element_type=F32)
    return h, m, (
        jnp.where(low, y[0:16, 0:128], y[16:32, 0:128]),
        jnp.where(low, y[32:48, 128:256], y[48:64, 128:256]),
    )


def store_half(half, low, h, m, first, second):
    b = h * 256 + m
    half[b], half[b + 128] = doubled(low, first)
    half[b + 1], half[b + 129] = doubled(low, second)


def finish_one(refs, low, h, m, sums):
    cheb, half = refs
    p = h * 128 + m
    cheb[p], cheb[p + 1] = sums
    store_half(half, low, h, m, *sums)


def finish_two(refs, low, h, m, sums):
    mixed, cheb, blend, half = refs
    p = h * 128 + m
    second = []
    for d in range(2):
        at = mixed[p + d]
        second.append(2.0 * sums[d] - at)
        blend[p + d] = 0.75 * at + 0.375 * cheb[p + d] + 0.5 * sums[d]
    store_half(half, low, h, m, *second)


def finish_three(refs, low, h, m, sums):
    blend, lag, out, room = refs[:4]
    slot = refs[4]
    p = h * 128 + m
    filtered = [blend[p + d] + 0.25 * sums[d] for d in range(2)]
    natural = swap_pair(low, *filtered)
    for d in range(2):
        t = h * 128 + lax.div(m, 2) + 64 * d
        cols = pl.ds(pl.multiple_of(t * LANES, LANES), LANES)
        room[slot + d] = natural[d]
        total = lag[0:1, cols] * natural[d][0:8]
        for l in range(1, lag.shape[0]):
            total = total + lag[l : l + 1, cols] * room[slot + d, l : l + 8, :]
        out[:, cols] = total


EDGE_GROUPS = 8
UNROLL = 14


def run_inner(body):
    def step(i, carry):
        for j in range(UNROLL):
            body(EDGE_GROUPS + i * UNROLL + j, j)
        return carry

    lax.fori_loop(0, (128 - 2 * EDGE_GROUPS) // UNROLL, step, 0)


def run_edge(body):
    for j in range(EDGE_GROUPS):
        body(j, j)
        body(128 - EDGE_GROUPS + j, EDGE_GROUPS + j)


def pass_call(kernel, cols, weights, half, halos, extra, held, new, edges, scratch, name):
    inputs = [cols, weights, half, *halos, *extra, *held]
    shapes = list(new) if not held else list(new)
    aliases = {3 + len(halos) + len(extra) + i: i for i in range(len(held))}
    sent = [jax.ShapeDtypeStruct((EDGE, 16, LANES), BF16)] * edges
    return pl.pallas_call(
        kernel,
        out_shape=tuple(shapes + sent),
        in_specs=[SSPEC] + [VSPEC] * (len(inputs) - 1),
        out_specs=(VSPEC,) * (len(shapes) + edges),
        scratch_shapes=scratch,
        input_output_aliases=aliases,
        compiler_params=pltpu.CompilerParams(vmem_limit_bytes=8 << 20),
        cost_estimate=pl.CostEstimate(
            flops=(1 << 30) if not held else (1 << 26), bytes_accessed=(16 << 20) if not held else (1 << 20), transcendentals=0
        ),
        name=name,
    )(inputs[0], *[in_vmem(x) for x in inputs[1:]])


def send_edges(half, lo, hi):
    lo[...] = half[0:EDGE]
    hi[...] = half[512 - EDGE : 512]


def inner_one(cols, weights, half, cheb, out_half):
    low = lane_bits(16) < HALF

    def body(g, j):
        h, m, sums = group_product(g, cols, weights, half, low)
        finish_one((cheb, out_half), low, h, m, sums)

    run_inner(body)


def edge_one(cols, weights, half, below, above, cheb_in, half_in, cheb, out_half, lo, hi):
    low = lane_bits(16) < HALF

    def body(g, j):
        h, m, sums = group_product(g, cols, weights, half, low, below, above)
        finish_one((cheb, out_half), low, h, m, sums)

    run_edge(body)
    send_edges(out_half, lo, hi)


def inner_two(cols, weights, half, mixed, cheb, blend, out_half):
    low = lane_bits(16) < HALF

    def body(g, j):
        h, m, sums = group_product(g, cols, weights, half, low)
        finish_two((mixed, cheb, blend, out_half), low, h, m, sums)

    run_inner(body)


def edge_two(cols, weights, half, below, above, mixed, cheb, blend_in, half_in, blend, out_half, lo, hi):
    low = lane_bits(16) < HALF

    def body(g, j):
        h, m, sums = group_product(g, cols, weights, half, low, below, above)
        finish_two((mixed, cheb, blend, out_half), low, h, m, sums)

    run_edge(body)
    send_edges(out_half, lo, hi)


def inner_three(cols, weights, half, blend, lag, out, room):
    low = lane_bits(16) < HALF

    def body(g, j):
        h, m, sums = group_product(g, cols, weights, half, low)
        finish_three((blend, lag, out, room, 2 * j), low, h, m, sums)

    run_inner(body)


def edge_three(cols, weights, half, below, above, blend, lag, out_in, out, room):
    low = lane_bits(16) < HALF

    def body(g, j):
        h, m, sums = group_product(g, cols, weights, half, low, below, above)
        finish_three((blend, lag, out, room, 2 * j), low, h, m, sums)

    run_edge(body)


def passed_along(value, axis, by):
    peers = lax.axis_size(axis)
    return lax.ppermute(value, axis, [(i, (i + by) % peers) for i in range(peers)])


def per_device(noise, lag, blocks, block_cols):
    count = blocks.shape[0]
    cols = block_cols.T - lax.axis_index("mesh") * count
    sent = noise.astype(BF16)
    prev = passed_along(sent, "tm", 1)
    following = passed_along(sent, "tm", -1)
    weights = repack(blocks)
    mixed, half, lo, hi = mix(in_vmem(noise), in_vmem(prev), in_vmem(following), in_vmem(lag))

    field = pltpu.VMEM(mixed.shape, F32)
    packed = pltpu.VMEM(half.shape, BF16)
    result = pltpu.VMEM(noise.shape, F32)
    room = [pltpu.VMEM((2 * UNROLL, 16, LANES), F32)]
    edge_room = [pltpu.VMEM((4 * EDGE_GROUPS, 16, LANES), F32)]

    halos = (passed_along(hi, "mesh", 1), passed_along(lo, "mesh", -1))
    held = pass_call(inner_one, cols, weights, half, (), (), (), (field, packed), 0, [], "inner_one")
    cheb, half, lo, hi = pass_call(
        edge_one, cols, weights, half, halos, (), held, (field, packed), 2, [], "edge_one"
    )
    halos = (passed_along(hi, "mesh", 1), passed_along(lo, "mesh", -1))
    held = pass_call(inner_two, cols, weights, half, (), (mixed, cheb), (), (field, packed), 0, [], "inner_two")
    blend, half, lo, hi = pass_call(
        edge_two, cols, weights, half, halos, (mixed, cheb), held, (field, packed), 2, [], "edge_two"
    )
    halos = (passed_along(hi, "mesh", 1), passed_along(lo, "mesh", -1))
    held = pass_call(inner_three, cols, weights, half, (), (blend, lag), (), (result,), 0, room, "inner_three")
    (out,) = pass_call(
        edge_three, cols, weights, half, halos, (blend, lag), held, (result,), 0, edge_room, "edge_three"
    )
    return out


def solution(mesh):
    placed = (P("tm", "mesh"), P(None, "mesh"), P("mesh", None, None, None), P("mesh", None))
    return jax.shard_map(
        per_device, mesh=mesh, in_specs=placed, out_specs=P("tm", "mesh"), check_vma=False
    )
```

```python
import functools

import jax
import jax.numpy as jnp
from jax import lax
from jax.experimental import pallas as pl
from jax.experimental.pallas import tpu as pltpu
from jax.sharding import PartitionSpec as P

LANES = 128
HALF = 64
EDGE = 16
F32 = jnp.float32
BF16 = jnp.bfloat16
VSPEC = pl.BlockSpec(memory_space=pltpu.VMEM)
SSPEC = pl.BlockSpec(memory_space=pltpu.SMEM)
ASPEC = pl.BlockSpec(memory_space=pl.ANY)


def in_vmem(x):
    return pltpu.with_memory_space_constraint(x, pltpu.VMEM)


def lane_bits(rows):
    return lax.broadcasted_iota(jnp.int32, (rows, LANES), 1)


def repack_kernel(src, out, held, stage, sems):
    ks, width, depth, blocks = src.shape
    deep = depth // 16
    halves = blocks // (2 * LANES)
    units = ks * deep
    slots = held.shape[0]

    def place(u):
        return lax.div(u, deep), pl.multiple_of(lax.rem(u, deep) * 16, 16)

    def fetch(u):
        k, j = place(u)
        slot = lax.rem(u, slots)
        return pltpu.make_async_copy(src.at[k, :, pl.ds(j, 16), :], held.at[slot], sems.at[slot])

    lane = lane_bits(16)
    masks = [(lane & (1 << s)) != 0 for s in range(7)]

    for u in range(slots - 1):
        fetch(u).start()

    def unit(u, carry):
        slot = lax.rem(u, slots)

        @pl.when(u + slots - 1 < units)
        def _():
            fetch(u + slots - 1).start()

        fetch(u).wait()
        k, j = place(u)
        row = pl.multiple_of(k * depth + j, 16)
        for h in range(halves):
            for r in range(8):
                vals = []
                for q in range(16):
                    n = r + 8 * q
                    at = LANES * (2 * h + n // 64)
                    v = held[slot, n % 64, :, at : at + LANES]
                    vals.append(pltpu.roll(v, n, 1) if n else v)
                for s in range(4):
                    vals = [jnp.where(masks[3 + s], vals[(q + (1 << s)) % 16], vals[q]) for q in range(16)]
                for q in range(16):
                    stage[h, r + 8 * q] = vals[q]
        for h in range(halves):
            for c in range(8):
                vals = [stage[h, (16 * c + q) % 128] for q in range(23)]
                vals = [jnp.where(masks[2], vals[q + 4], vals[q]) for q in range(19)]
                vals = [jnp.where(masks[1], vals[q + 2], vals[q]) for q in range(17)]
                vals = [jnp.where(masks[0], vals[q + 1], vals[q]) for q in range(16)]
                for q in range(16):
                    n = 16 * c + q
                    m = (128 - n) % 128
                    out[h, m, pl.ds(row, 16), :] = pltpu.roll(vals[q], n, 1) if n else vals[q]
        return carry

    lax.fori_loop(0, units, unit, 0)


def repack(blocks):
    src = pltpu.with_memory_space_constraint(jnp.transpose(blocks, (1, 2, 3, 0)), pltpu.HBM)
    ks, width, depth, count = src.shape
    slots = 4
    return pl.pallas_call(
        repack_kernel,
        out_shape=pltpu.VMEM((count // 256, LANES, ks * depth, LANES), BF16),
        in_specs=[ASPEC],
        out_specs=VSPEC,
        scratch_shapes=[
            pltpu.VMEM((slots, width, 16, count), BF16),
            pltpu.VMEM((count // 256, LANES, 16, LANES), BF16),
            pltpu.SemaphoreType.DMA((slots,)),
        ],
        compiler_params=pltpu.CompilerParams(vmem_limit_bytes=10 << 20),
        cost_estimate=pl.CostEstimate(flops=0, bytes_accessed=40 << 20, transcendentals=0),
        name="repack",
    )(src)


def swap_pair(low, first, second):
    return (
        jnp.where(low, first, pltpu.roll(second, HALF, 1)),
        jnp.where(low, pltpu.roll(first, HALF, 1), second),
    )


def doubled(low, tile):
    turned = pltpu.roll(tile, HALF, 1)
    return jnp.where(low, tile, turned).astype(BF16), jnp.where(low, turned, tile).astype(BF16)


def mix_kernel(noise, prev, following, lag, weights, mixed, half, lo, hi, ext):
    lags = lag.shape[0]
    steps = noise.shape[0]
    low = lane_bits(2 * steps) < HALF

    def tile(t, slot):
        cols = pl.ds(pl.multiple_of(t * LANES, LANES), LANES)
        ext[slot, 0:8, :] = prev[:, cols].astype(F32)
        ext[slot, 8:16, :] = noise[:, cols]
        ext[slot, 16:24, :] = following[:, cols].astype(F32)
        total = lag[0:1, cols] * ext[slot, 8:24, :]
        for l in range(1, lags):
            total = total + lag[l : l + 1, cols] * ext[slot, 8 - l : 24 - l, :]
        return total

    def step(i, carry):
        for j in range(4):
            g = i * 4 + j
            h = lax.div(g, 64)
            m = 2 * lax.rem(g, 64)
            t = h * 128 + lax.rem(g, 64)
            first = tile(t, 2 * j)
            second = tile(t + 64, 2 * j + 1)
            b = h * 256 + m
            half[b], half[b + 1] = doubled(low, first)
            half[b + 128], half[b + 129] = doubled(low, second)
            p = h * 128 + m
            mixed[p], mixed[p + 1] = swap_pair(low, first, second)
        return carry

    lax.fori_loop(0, 32, step, 0)
    lo[...] = half[0:EDGE]
    hi[...] = half[512 - EDGE : 512]


def mix(noise, prev, following, lag, weights):
    rows = 2 * noise.shape[0]
    tiles = noise.shape[1] // LANES
    return pl.pallas_call(
        mix_kernel,
        out_shape=(
            pltpu.VMEM((tiles, rows, LANES), F32),
            pltpu.VMEM((2 * tiles, rows, LANES), BF16),
            jax.ShapeDtypeStruct((EDGE, rows, LANES), BF16),
            jax.ShapeDtypeStruct((EDGE, rows, LANES), BF16),
        ),
        in_specs=[VSPEC] * 5,
        out_specs=(VSPEC,) * 4,
        scratch_shapes=[pltpu.VMEM((8, 24, LANES), F32)],
        compiler_params=pltpu.CompilerParams(vmem_limit_bytes=8 << 20),
        cost_estimate=pl.CostEstimate(flops=8 << 20, bytes_accessed=8 << 20, transcendentals=0),
        name="mix",
    )(*[in_vmem(x) for x in (noise, prev, following, lag, weights)])


def group_product(g, cols, weights, half, low, below=None, above=None):
    h = lax.div(g, 64)
    m = 2 * lax.rem(g, 64)
    rows = []
    for j in range(4):
        b = h * 256 + (j % 2) * 128 + m + j // 2
        picked = []
        for k in range(4):
            c = cols[k, b]
            if below is None or k != 1:
                picked.append(half[c])
            else:
                own = half[jnp.clip(c, 0, 511)]
                under = below[jnp.clip(c + EDGE, 0, EDGE - 1)]
                over = above[jnp.clip(c - 512, 0, EDGE - 1)]
                picked.append(jnp.where(c < 0, under, jnp.where(c >= 512, over, own)))
        left = jnp.where(low, picked[0], picked[1])
        right = jnp.where(low, picked[2], picked[3])
        rows.append(jnp.concatenate([left, right], axis=1))
    taken = jnp.concatenate(rows, axis=0)
    tile = jnp.concatenate([weights[h, m], weights[h, m + 1]], axis=1)
    y = jnp.dot(taken, tile, preferred_element_type=F32)
    return h, m, (
        jnp.where(low, y[0:16, 0:128], y[16:32, 0:128]),
        jnp.where(low, y[32:48, 128:256], y[48:64, 128:256]),
    )


def store_half(half, low, h, m, first, second):
    b = h * 256 + m
    half[b], half[b + 128] = doubled(low, first)
    half[b + 1], half[b + 129] = doubled(low, second)


def finish_one(refs, low, h, m, sums):
    cheb, half = refs
    p = h * 128 + m
    cheb[p], cheb[p + 1] = sums
    store_half(half, low, h, m, *sums)


def finish_two(refs, low, h, m, sums):
    mixed, cheb, blend, half = refs
    p = h * 128 + m
    second = []
    for d in range(2):
        at = mixed[p + d]
        second.append(2.0 * sums[d] - at)
        blend[p + d] = 0.75 * at + 0.375 * cheb[p + d] + 0.5 * sums[d]
    store_half(half, low, h, m, *second)


def finish_three(refs, low, h, m, sums):
    blend, lag, out, room = refs[:4]
    slot = refs[4]
    p = h * 128 + m
    filtered = [blend[p + d] + 0.25 * sums[d] for d in range(2)]
    natural = swap_pair(low, *filtered)
    for d in range(2):
        t = h * 128 + lax.div(m, 2) + 64 * d
        cols = pl.ds(pl.multiple_of(t * LANES, LANES), LANES)
        room[slot + d] = natural[d]
        total = lag[0:1, cols] * natural[d][0:8]
        for l in range(1, lag.shape[0]):
            total = total + lag[l : l + 1, cols] * room[slot + d, l : l + 8, :]
        out[:, cols] = total


EDGE_GROUPS = 8
UNROLL = 14


def run_inner(body):
    def step(i, carry):
        for j in range(UNROLL):
            body(EDGE_GROUPS + i * UNROLL + j, j)
        return carry

    lax.fori_loop(0, (128 - 2 * EDGE_GROUPS) // UNROLL, step, 0)


def run_edge(body):
    for j in range(EDGE_GROUPS):
        body(j, j)
        body(128 - EDGE_GROUPS + j, EDGE_GROUPS + j)


def pass_call(kernel, cols, weights, half, halos, extra, held, new, edges, scratch, name):
    inputs = [cols, weights, half, *halos, *extra, *held]
    shapes = list(new) if not held else list(new)
    aliases = {3 + len(halos) + len(extra) + i: i for i in range(len(held))}
    sent = [jax.ShapeDtypeStruct((EDGE, 16, LANES), BF16)] * edges
    return pl.pallas_call(
        kernel,
        out_shape=tuple(shapes + sent),
        in_specs=[SSPEC] + [VSPEC] * (len(inputs) - 1),
        out_specs=(VSPEC,) * (len(shapes) + edges),
        scratch_shapes=scratch,
        input_output_aliases=aliases,
        compiler_params=pltpu.CompilerParams(vmem_limit_bytes=8 << 20),
        cost_estimate=pl.CostEstimate(
            flops=(1 << 30) if not held else (1 << 26), bytes_accessed=(16 << 20) if not held else (1 << 20), transcendentals=0
        ),
        name=name,
    )(inputs[0], *[in_vmem(x) for x in inputs[1:]])


def send_edges(half, lo, hi):
    lo[...] = half[0:EDGE]
    hi[...] = half[512 - EDGE : 512]


def inner_one(cols, weights, half, cheb, out_half):
    low = lane_bits(16) < HALF

    def body(g, j):
        h, m, sums = group_product(g, cols, weights, half, low)
        finish_one((cheb, out_half), low, h, m, sums)

    run_inner(body)


def edge_one(cols, weights, half, below, above, cheb_in, half_in, cheb, out_half, lo, hi):
    low = lane_bits(16) < HALF

    def body(g, j):
        h, m, sums = group_product(g, cols, weights, half, low, below, above)
        finish_one((cheb, out_half), low, h, m, sums)

    run_edge(body)
    send_edges(out_half, lo, hi)


def inner_two(cols, weights, half, mixed, cheb, blend, out_half):
    low = lane_bits(16) < HALF

    def body(g, j):
        h, m, sums = group_product(g, cols, weights, half, low)
        finish_two((mixed, cheb, blend, out_half), low, h, m, sums)

    run_inner(body)


def edge_two(cols, weights, half, below, above, mixed, cheb, blend_in, half_in, blend, out_half, lo, hi):
    low = lane_bits(16) < HALF

    def body(g, j):
        h, m, sums = group_product(g, cols, weights, half, low, below, above)
        finish_two((mixed, cheb, blend, out_half), low, h, m, sums)

    run_edge(body)
    send_edges(out_half, lo, hi)


def inner_three(cols, weights, half, blend, lag, out, room):
    low = lane_bits(16) < HALF

    def body(g, j):
        h, m, sums = group_product(g, cols, weights, half, low)
        finish_three((blend, lag, out, room, 2 * j), low, h, m, sums)

    run_inner(body)


def edge_three(cols, weights, half, below, above, blend, lag, out_in, out, room):
    low = lane_bits(16) < HALF

    def body(g, j):
        h, m, sums = group_product(g, cols, weights, half, low, below, above)
        finish_three((blend, lag, out, room, 2 * j), low, h, m, sums)

    run_edge(body)


def passed_along(value, axis, by):
    peers = lax.axis_size(axis)
    return lax.ppermute(value, axis, [(i, (i + by) % peers) for i in range(peers)])


def per_device(noise, lag, blocks, block_cols):
    count = blocks.shape[0]
    cols = block_cols.T - lax.axis_index("mesh") * count
    sent = noise.astype(BF16)
    prev = passed_along(sent, "tm", 1)
    following = passed_along(sent, "tm", -1)
    weights = repack(blocks)
    mixed, half, lo, hi = mix(noise, prev, following, lag, weights)

    field = pltpu.VMEM(mixed.shape, F32)
    packed = pltpu.VMEM(half.shape, BF16)
    result = pltpu.VMEM(noise.shape, F32)
    room = [pltpu.VMEM((2 * UNROLL, 16, LANES), F32)]
    edge_room = [pltpu.VMEM((4 * EDGE_GROUPS, 16, LANES), F32)]

    halos = (passed_along(hi, "mesh", 1), passed_along(lo, "mesh", -1))
    held = pass_call(inner_one, cols, weights, half, (), (), (), (field, packed), 0, [], "inner_one")
    cheb, half, lo, hi = pass_call(
        edge_one, cols, weights, half, halos, (), held, (field, packed), 2, [], "edge_one"
    )
    halos = (passed_along(hi, "mesh", 1), passed_along(lo, "mesh", -1))
    held = pass_call(inner_two, cols, weights, half, (), (mixed, cheb), (), (field, packed), 0, [], "inner_two")
    blend, half, lo, hi = pass_call(
        edge_two, cols, weights, half, halos, (mixed, cheb), held, (field, packed), 2, [], "edge_two"
    )
    halos = (passed_along(hi, "mesh", 1), passed_along(lo, "mesh", -1))
    held = pass_call(inner_three, cols, weights, half, (), (blend, lag), (), (result,), 0, room, "inner_three")
    (out,) = pass_call(
        edge_three, cols, weights, half, halos, (blend, lag), held, (result,), 0, edge_room, "edge_three"
    )
    return out


def solution(mesh):
    placed = (P("tm", "mesh"), P(None, "mesh"), P("mesh", None, None, None), P("mesh", None))
    return jax.shard_map(
        per_device, mesh=mesh, in_specs=placed, out_specs=P("tm", "mesh"), check_vma=False
    )
```

```python
import functools

import jax
import jax.numpy as jnp
from jax import lax
from jax.experimental import pallas as pl
from jax.experimental.pallas import tpu as pltpu
from jax.sharding import PartitionSpec as P

LANES = 128
HALF = 64
EDGE = 16
F32 = jnp.float32
BF16 = jnp.bfloat16
VSPEC = pl.BlockSpec(memory_space=pltpu.VMEM)
SSPEC = pl.BlockSpec(memory_space=pltpu.SMEM)
ASPEC = pl.BlockSpec(memory_space=pl.ANY)


def in_vmem(x):
    return pltpu.with_memory_space_constraint(x, pltpu.VMEM)


def lane_bits(rows):
    return lax.broadcasted_iota(jnp.int32, (rows, LANES), 1)


def repack_kernel(src, cols, out, held, stage, sems):
    ks, width, depth, blocks = src.shape
    deep = depth // 16
    units = ks * deep
    slots = held.shape[0]

    def place(u):
        return lax.div(u, deep), pl.multiple_of(lax.rem(u, deep) * 16, 16)

    def fetch(u):
        k, j = place(u)
        slot = lax.rem(u, slots)
        return pltpu.make_async_copy(src.at[k, :, pl.ds(j, 16), :], held.at[slot], sems.at[slot])

    lane = lax.broadcasted_iota(jnp.int32, (16, 2 * LANES), 1)
    masks = [(lane & (1 << s)) != 0 for s in range(7)]

    for u in range(slots - 1):
        fetch(u).start()

    def unit(u, carry):
        slot = lax.rem(u, slots)

        @pl.when(u + slots - 1 < units)
        def _():
            fetch(u + slots - 1).start()

        fetch(u).wait()
        k, j = place(u)
        row = pl.multiple_of(k * depth + j, 16)
        for r in range(8):
            vals = []
            for q in range(16):
                n = r + 8 * q
                at = 2 * LANES * (n // 64)
                v = held[slot, n % 64, :, at : at + 2 * LANES]
                vals.append(pltpu.roll(v, n, 1) if n else v)
            for s in range(4):
                vals = [jnp.where(masks[3 + s], vals[(q + (1 << s)) % 16], vals[q]) for q in range(16)]
            for q in range(16):
                stage[r + 8 * q] = vals[q]
        for c in range(16):
            vals = [stage[(8 * c + q) % 128] for q in range(15)]
            vals = [jnp.where(masks[2], vals[q + 4], vals[q]) for q in range(11)]
            vals = [jnp.where(masks[1], vals[q + 2], vals[q]) for q in range(9)]
            vals = [jnp.where(masks[0], vals[q + 1], vals[q]) for q in range(8)]
            for q in range(8):
                n = 8 * c + q
                out[(128 - n) % 128, pl.ds(row, 16), :] = pltpu.roll(vals[q], n + LANES, 1) if n else vals[q]
        return carry

    lax.fori_loop(0, units, unit, 0)


def repack(blocks, cols):
    src = pltpu.with_memory_space_constraint(jnp.transpose(blocks, (1, 2, 3, 0)), pltpu.HBM)
    ks, width, depth, count = src.shape
    slots = 4
    return pl.pallas_call(
        repack_kernel,
        out_shape=pltpu.VMEM((LANES, ks * depth, 2 * LANES), BF16),
        in_specs=[ASPEC, SSPEC],
        out_specs=VSPEC,
        scratch_shapes=[
            pltpu.VMEM((slots, width, 16, count), BF16),
            pltpu.VMEM((LANES, 16, 2 * LANES), BF16),
            pltpu.SemaphoreType.DMA((slots,)),
        ],
        compiler_params=pltpu.CompilerParams(vmem_limit_bytes=10 << 20),
        cost_estimate=pl.CostEstimate(flops=0, bytes_accessed=40 << 20, transcendentals=0),
        name="repack",
    )(src, cols)


def swap_pair(low, first, second):
    return (
        jnp.where(low, first, pltpu.roll(second, HALF, 1)),
        jnp.where(low, pltpu.roll(first, HALF, 1), second),
    )


def doubled(low, tile):
    turned = pltpu.roll(tile, HALF, 1)
    return [
        jnp.concatenate([t[0:8], t[8:16]], axis=1).astype(BF16)
        for t in (jnp.where(low, tile, turned), jnp.where(low, turned, tile))
    ]


def mix_kernel(noise, prev, following, lag, weights, mixed, half, lo, hi, ext):
    lags = lag.shape[0]
    steps = noise.shape[0]
    low = lane_bits(2 * steps) < HALF

    def tile(t, slot):
        cols = pl.ds(pl.multiple_of(t * LANES, LANES), LANES)
        ext[slot, 0:8, :] = prev[:, cols].astype(F32)
        ext[slot, 8:16, :] = noise[:, cols]
        ext[slot, 16:24, :] = following[:, cols].astype(F32)
        total = lag[0:1, cols] * ext[slot, 8:24, :]
        for l in range(1, lags):
            total = total + lag[l : l + 1, cols] * ext[slot, 8 - l : 24 - l, :]
        return total

    def step(i, carry):
        for j in range(8):
            g = i * 8 + j
            h = lax.div(g, 64)
            m = 2 * lax.rem(g, 64)
            first = tile(g, 2 * j)
            second = tile(g + 128, 2 * j + 1)
            b = h * 128 + m
            half[b], half[b + 1] = doubled(low, first)
            half[b + 256], half[b + 257] = doubled(low, second)
            mixed[m, h], mixed[m + 1, h] = swap_pair(low, first, second)
        return carry

    lax.fori_loop(0, 16, step, 0)
    lo[...] = half[0:EDGE]
    hi[...] = half[512 - EDGE : 512]


def mix(noise, prev, following, lag, weights):
    rows = 2 * noise.shape[0]
    tiles = noise.shape[1] // LANES
    return pl.pallas_call(
        mix_kernel,
        out_shape=(
            pltpu.VMEM((tiles // 2, 2, rows, LANES), F32),
            pltpu.VMEM((2 * tiles, 8, 2 * LANES), BF16),
            jax.ShapeDtypeStruct((EDGE, 8, 2 * LANES), BF16),
            jax.ShapeDtypeStruct((EDGE, 8, 2 * LANES), BF16),
        ),
        in_specs=[VSPEC] * 5,
        out_specs=(VSPEC,) * 4,
        scratch_shapes=[pltpu.VMEM((16, 24, LANES), F32)],
        compiler_params=pltpu.CompilerParams(vmem_limit_bytes=8 << 20),
        cost_estimate=pl.CostEstimate(flops=8 << 20, bytes_accessed=8 << 20, transcendentals=0),
        name="mix",
    )(*[in_vmem(x) for x in (noise, prev, following, lag, weights)])


def group_product(m, cols, weights, half, low, below=None, above=None):
    rows = []
    for j in range(4):
        b = (j % 2) * 256 + (j // 2) * 128 + m
        picked = []
        for k in range(4):
            c = cols[k, b]
            if below is None or k != 1:
                picked.append(half[c])
            else:
                own = half[jnp.clip(c, 0, 511)]
                under = below[jnp.clip(c + EDGE, 0, EDGE - 1)]
                over = above[jnp.clip(c - 512, 0, EDGE - 1)]
                picked.append(jnp.where(c < 0, under, jnp.where(c >= 512, over, own)))
        left = jnp.where(low, picked[0], picked[1])
        right = jnp.where(low, picked[2], picked[3])
        rows.append(jnp.concatenate([left[:, :LANES], right[:, :LANES]], axis=1))
        rows.append(jnp.concatenate([left[:, LANES:], right[:, LANES:]], axis=1))
    taken = jnp.concatenate(rows, axis=0)
    y = jnp.dot(taken, weights[m], preferred_element_type=F32)
    low = low[:, :LANES]
    low = jnp.concatenate([low, low], axis=0)
    return (
        jnp.where(low, y[0:16, 0:128], y[16:32, 0:128]),
        jnp.where(low, y[32:48, 128:256], y[48:64, 128:256]),
    )


def masks():
    both = (lax.broadcasted_iota(jnp.int32, (8, 2 * LANES), 1) & HALF) == 0
    return both, lane_bits(16) < HALF


def store_half(half, low, m, pairs):
    for h in range(2):
        b = h * 128 + m
        half[b], half[b + 256] = doubled(low, pairs[h])


def finish_one(refs, low, m, sums):
    cheb, half = refs
    for h in range(2):
        cheb[m, h] = sums[h]
    store_half(half, low, m, sums)


def finish_two(refs, low, m, sums):
    mixed, cheb, blend, half = refs
    second = []
    for h in range(2):
        at = mixed[m, h]
        second.append(2.0 * sums[h] - at)
        blend[m, h] = 0.75 * at + 0.375 * cheb[m, h] + 0.5 * sums[h]
    store_half(half, low, m, second)


def finish_three(refs, low, u, filtered):
    lag, out, room, slot = refs
    for h in range(2):
        natural = swap_pair(low, filtered[0][h], filtered[1][h])
        for d in range(2):
            at = slot + 2 * h + d
            room[at] = natural[d]
            cols = pl.ds(pl.multiple_of((h * 64 + u + 128 * d) * LANES, LANES), LANES)
            total = lag[0:1, cols] * natural[d][0:8]
            for l in range(1, lag.shape[0]):
                total = total + lag[l : l + 1, cols] * room[at, l : l + 8, :]
            out[:, cols] = total


EDGE_UNITS = 8
UNROLL = 16


def run_inner(body):
    def step(i, carry):
        for j in range(UNROLL):
            body(EDGE_UNITS + i * UNROLL + j, j)
        return carry

    lax.fori_loop(0, (64 - 2 * EDGE_UNITS) // UNROLL, step, 0)


def run_edge(body):
    for j in range(EDGE_UNITS):
        body(j, j)
        body(64 - EDGE_UNITS + j, EDGE_UNITS + j)


def pass_call(kernel, cols, weights, half, halos, extra, held, new, edges, scratch, name):
    inputs = [cols, weights, half, *halos, *extra, *held]
    shapes = list(new) if not held else list(new)
    aliases = {3 + len(halos) + len(extra) + i: i for i in range(len(held))}
    sent = [jax.ShapeDtypeStruct((EDGE, 8, 2 * LANES), BF16)] * edges
    return pl.pallas_call(
        kernel,
        out_shape=tuple(shapes + sent),
        in_specs=[SSPEC] + [VSPEC] * (len(inputs) - 1),
        out_specs=(VSPEC,) * (len(shapes) + edges),
        scratch_shapes=scratch,
        input_output_aliases=aliases,
        compiler_params=pltpu.CompilerParams(vmem_limit_bytes=8 << 20),
        cost_estimate=pl.CostEstimate(
            flops=(1 << 30) if not held else (1 << 26), bytes_accessed=(16 << 20) if not held else (1 << 20), transcendentals=0
        ),
        name=name,
    )(inputs[0], *[in_vmem(x) for x in inputs[1:]])


def send_edges(half, lo, hi):
    lo[...] = half[0:EDGE]
    hi[...] = half[512 - EDGE : 512]


def inner_one(cols, weights, half, cheb, out_half):
    both, low = masks()

    def body(u, j):
        for d in range(2):
            m = 2 * u + d
            sums = group_product(m, cols, weights, half, both)
            finish_one((cheb, out_half), low, m, sums)

    run_inner(body)


def edge_one(cols, weights, half, below, above, cheb_in, half_in, cheb, out_half, lo, hi):
    both, low = masks()

    def body(u, j):
        for d in range(2):
            m = 2 * u + d
            sums = group_product(m, cols, weights, half, both, below, above)
            finish_one((cheb, out_half), low, m, sums)

    run_edge(body)
    send_edges(out_half, lo, hi)


def inner_two(cols, weights, half, mixed, cheb, blend, out_half):
    both, low = masks()

    def body(u, j):
        for d in range(2):
            m = 2 * u + d
            sums = group_product(m, cols, weights, half, both)
            finish_two((mixed, cheb, blend, out_half), low, m, sums)

    run_inner(body)


def edge_two(cols, weights, half, below, above, mixed, cheb, blend_in, half_in, blend, out_half, lo, hi):
    both, low = masks()

    def body(u, j):
        for d in range(2):
            m = 2 * u + d
            sums = group_product(m, cols, weights, half, both, below, above)
            finish_two((mixed, cheb, blend, out_half), low, m, sums)

    run_edge(body)
    send_edges(out_half, lo, hi)


def inner_three(cols, weights, half, blend, lag, out, room):
    both, low = masks()

    def body(u, j):
        filtered = []
        for d in range(2):
            m = 2 * u + d
            sums = group_product(m, cols, weights, half, both)
            filtered.append([blend[m, h] + 0.25 * sums[h] for h in range(2)])
        finish_three((lag, out, room, 4 * j), low, u, filtered)

    run_inner(body)


def edge_three(cols, weights, half, below, above, blend, lag, out_in, out, room):
    both, low = masks()

    def body(u, j):
        filtered = []
        for d in range(2):
            m = 2 * u + d
            sums = group_product(m, cols, weights, half, both, below, above)
            filtered.append([blend[m, h] + 0.25 * sums[h] for h in range(2)])
        finish_three((lag, out, room, 4 * j), low, u, filtered)

    run_edge(body)


def passed_along(value, axis, by, wraps):
    peers = lax.axis_size(axis)
    pairs = [(i, (i + by) % peers) for i in range(peers) if wraps or 0 <= i + by < peers]
    return lax.ppermute(value, axis, pairs)


def per_device(noise, lag, blocks, block_cols):
    count = blocks.shape[0]
    cols = block_cols.T - lax.axis_index("mesh") * count
    sent = noise.astype(BF16)
    following = passed_along(sent, "tm", -1, True)
    prev = passed_along(sent, "tm", 1, True)
    weights = repack(blocks, cols)
    mixed, half, lo, hi = mix(noise, prev, following, lag, weights)

    field = pltpu.VMEM(mixed.shape, F32)
    packed = pltpu.VMEM(half.shape, BF16)
    result = pltpu.VMEM(noise.shape, F32)
    room = [pltpu.VMEM((4 * UNROLL, 16, LANES), F32)]
    edge_room = [pltpu.VMEM((8 * EDGE_UNITS, 16, LANES), F32)]

    halos = (passed_along(hi, "mesh", 1, True), passed_along(lo, "mesh", -1, True))
    held = pass_call(inner_one, cols, weights, half, (), (), (), (field, packed), 0, [], "inner_one")
    cheb, half, lo, hi = pass_call(
        edge_one, cols, weights, half, halos, (), held, (field, packed), 2, [], "edge_one"
    )
    halos = (passed_along(hi, "mesh", 1, True), passed_along(lo, "mesh", -1, True))
    held = pass_call(inner_two, cols, weights, half, (), (mixed, cheb), (), (field, packed), 0, [], "inner_two")
    blend, half, lo, hi = pass_call(
        edge_two, cols, weights, half, halos, (mixed, cheb), held, (field, packed), 2, [], "edge_two"
    )
    halos = (passed_along(hi, "mesh", 1, True), passed_along(lo, "mesh", -1, True))
    held = pass_call(inner_three, cols, weights, half, (), (blend, lag), (), (result,), 0, room, "inner_three")
    (out,) = pass_call(
        edge_three, cols, weights, half, halos, (blend, lag), held, (result,), 0, edge_room, "edge_three"
    )
    return out


def solution(mesh):
    placed = (P("tm", "mesh"), P(None, "mesh"), P("mesh", None, None, None), P("mesh", None))
    return jax.shard_map(
        per_device, mesh=mesh, in_specs=placed, out_specs=P("tm", "mesh"), check_vma=False
    )
```

```python
import functools

import jax
import jax.numpy as jnp
from jax import lax
from jax.experimental import pallas as pl
from jax.experimental.pallas import tpu as pltpu
from jax.sharding import PartitionSpec as P

LANES = 128
HALF = 64
EDGE = 16
PART = 512
F32 = jnp.float32
BF16 = jnp.bfloat16
VSPEC = pl.BlockSpec(memory_space=pltpu.VMEM)
SSPEC = pl.BlockSpec(memory_space=pltpu.SMEM)
ASPEC = pl.BlockSpec(memory_space=pl.ANY)


def in_vmem(x):
    return pltpu.with_memory_space_constraint(x, pltpu.VMEM)


def lane_bits(rows):
    return lax.broadcasted_iota(jnp.int32, (rows, LANES), 1)


def repack_kernel(src, out, held, stage, sems):
    ks, width, depth, blocks = src.shape
    deep = depth // 16
    units = ks * deep
    slots = held.shape[0]

    def place(u):
        return lax.div(u, deep), pl.multiple_of(lax.rem(u, deep) * 16, 16)

    def fetch(u):
        k, j = place(u)
        slot = lax.rem(u, slots)
        return pltpu.make_async_copy(src.at[k, :, pl.ds(j, 16), :], held.at[slot], sems.at[slot])

    lane = lax.broadcasted_iota(jnp.int32, (16, 2 * LANES), 1)
    masks = [(lane & (1 << s)) != 0 for s in range(7)]

    for u in range(slots - 1):
        fetch(u).start()

    def unit(u, carry):
        slot = lax.rem(u, slots)

        @pl.when(u + slots - 1 < units)
        def _():
            fetch(u + slots - 1).start()

        fetch(u).wait()
        k, j = place(u)
        row = pl.multiple_of(k * depth + j, 16)
        for r in range(8):
            vals = []
            for q in range(16):
                n = r + 8 * q
                at = 2 * LANES * (n // 64)
                v = held[slot, n % 64, :, at : at + 2 * LANES]
                if n:
                    v = jnp.concatenate([pltpu.roll(v[:, :LANES], n, 1), pltpu.roll(v[:, LANES:], n, 1)], axis=1)
                vals.append(v)
            for s in range(4):
                vals = [jnp.where(masks[3 + s], vals[(q + (1 << s)) % 16], vals[q]) for q in range(16)]
            for q in range(16):
                stage[r + 8 * q] = vals[q]
        for c in range(16):
            vals = [stage[(8 * c + q) % 128] for q in range(15)]
            vals = [jnp.where(masks[2], vals[q + 4], vals[q]) for q in range(11)]
            vals = [jnp.where(masks[1], vals[q + 2], vals[q]) for q in range(9)]
            vals = [jnp.where(masks[0], vals[q + 1], vals[q]) for q in range(8)]
            for q in range(8):
                n = 8 * c + q
                out[(128 - n) % 128, pl.ds(row, 16), :] = vals[q]
        return carry

    def two_units(i, carry):
        return unit(2 * i + 1, unit(2 * i, carry))

    lax.fori_loop(0, units // 2, two_units, 0)


def repack(blocks):
    src = pltpu.with_memory_space_constraint(jnp.transpose(blocks, (1, 2, 3, 0)), pltpu.HBM)
    ks, width, depth, count = src.shape
    slots = 4
    return pl.pallas_call(
        repack_kernel,
        out_shape=pltpu.VMEM((LANES, ks * depth, 2 * LANES), BF16),
        in_specs=[ASPEC],
        out_specs=VSPEC,
        scratch_shapes=[
            pltpu.VMEM((slots, width, 16, count), BF16),
            pltpu.VMEM((LANES, 16, 2 * LANES), BF16),
            pltpu.SemaphoreType.DMA((slots,)),
        ],
        compiler_params=pltpu.CompilerParams(vmem_limit_bytes=10 << 20),
        cost_estimate=pl.CostEstimate(flops=0, bytes_accessed=40 << 20, transcendentals=0),
        name="repack",
    )(src)


def swap_pair(low, first, second):
    return (
        jnp.where(low, first, pltpu.roll(second, HALF, 1)),
        jnp.where(low, pltpu.roll(first, HALF, 1), second),
    )


def doubled(low, tile):
    turned = pltpu.roll(tile, HALF, 1)
    return [
        jnp.concatenate([t[0:8], t[8:16]], axis=1).astype(BF16)
        for t in (jnp.where(low, tile, turned), jnp.where(low, turned, tile))
    ]


def mix_kernel(noise, following, prev, lag, weights, mixed, half, lo, hi, ext):
    lags = lag.shape[0]
    steps = noise.shape[0]
    low = lane_bits(2 * steps) < HALF

    def tile(t, slot):
        cols = pl.ds(pl.multiple_of(t * LANES, LANES), LANES)
        ext[slot, 0:8, :] = prev[:, cols].astype(F32)
        ext[slot, 8:16, :] = noise[:, cols]
        ext[slot, 16:24, :] = following[:, cols].astype(F32)
        total = lag[0:1, cols] * ext[slot, 8:24, :]
        for l in range(1, lags):
            total = total + lag[l : l + 1, cols] * ext[slot, 8 - l : 24 - l, :]
        return total

    def step(i, carry):
        for j in range(32):
            g = i * 32 + j
            h = lax.div(g, 64)
            m = 2 * lax.rem(g, 64)
            first = tile(g, 2 * j)
            second = tile(g + 128, 2 * j + 1)
            b = h * 128 + m
            half[b], half[b + 1] = doubled(low, first)
            half[b + 256], half[b + 257] = doubled(low, second)
            mixed[m, h], mixed[m + 1, h] = swap_pair(low, first, second)
        return carry

    lax.fori_loop(0, 4, step, 0)
    send_edges(half, lo, hi)


def mix(noise, following, prev, lag, weights):
    rows = 2 * noise.shape[0]
    tiles = noise.shape[1] // LANES
    return pl.pallas_call(
        mix_kernel,
        out_shape=(
            pltpu.VMEM((tiles // 2, 2, rows, LANES), F32),
            pltpu.VMEM((2 * tiles, 8, 2 * LANES), BF16),
            jax.ShapeDtypeStruct((EDGE, 8, 2 * LANES), BF16),
            jax.ShapeDtypeStruct((EDGE, 8, 2 * LANES), BF16),
        ),
        in_specs=[VSPEC] * 5,
        out_specs=(VSPEC,) * 4,
        scratch_shapes=[pltpu.VMEM((64, 24, LANES), F32)],
        compiler_params=pltpu.CompilerParams(vmem_limit_bytes=8 << 20),
        cost_estimate=pl.CostEstimate(flops=8 << 20, bytes_accessed=8 << 20, transcendentals=0),
        name="mix",
    )(*[in_vmem(x) for x in (noise, following, prev, lag, weights)])


def group_product(m, cols, weights, half, low, halo=None, row=None):
    rows = []
    for j in range(4):
        b = (j % 2) * 256 + (j // 2) * 128 + m
        picked = []
        for k in range(4):
            c = cols[k, b]
            value = half[c & (PART - 1)]
            if j == row and k == 1:
                near = (c ^ cols[0, b]) < PART
                value = jnp.where(near, value, halo[c & (EDGE - 1)])
            picked.append(value)
        left = jnp.where(low, picked[0], picked[1])
        right = jnp.where(low, picked[2], picked[3])
        rows.append(jnp.concatenate([left[:, :LANES], right[:, :LANES]], axis=1))
        rows.append(jnp.concatenate([left[:, LANES:], right[:, LANES:]], axis=1))
    taken = jnp.concatenate(rows, axis=0)
    y = jnp.dot(taken, weights[m], preferred_element_type=F32)
    turned = ((lane_bits(16) - m) & HALF) == 0
    back = (LANES - m) & (LANES - 1)
    return [
        pltpu.roll(jnp.where(turned, y[r : r + 16, at : at + LANES], y[r + 16 : r + 32, at : at + LANES]), back, 1)
        for r, at in ((0, 0), (32, LANES))
    ]


def masks():
    both = (lax.broadcasted_iota(jnp.int32, (8, 2 * LANES), 1) & HALF) == 0
    return both, lane_bits(16) < HALF


def store_half(half, low, m, pairs):
    for h in range(2):
        b = h * 128 + m
        half[b], half[b + 256] = doubled(low, pairs[h])


def finish_one(refs, low, m, sums):
    cheb, half = refs
    for h in range(2):
        cheb[m, h] = sums[h]
    store_half(half, low, m, sums)


def finish_two(refs, low, m, sums):
    mixed, cheb, blend, half = refs
    second = []
    for h in range(2):
        at = mixed[m, h]
        second.append(2.0 * sums[h] - at)
        blend[m, h] = 0.75 * at + 0.375 * cheb[m, h] + 0.5 * sums[h]
    store_half(half, low, m, second)


def finish_three(refs, low, u, filtered):
    lag, out, room, slot = refs
    for h in range(2):
        natural = swap_pair(low, filtered[0][h], filtered[1][h])
        for d in range(2):
            at = slot + 2 * h + d
            room[at] = natural[d]
            cols = pl.ds(pl.multiple_of((h * 64 + u + 128 * d) * LANES, LANES), LANES)
            total = lag[0:1, cols] * natural[d][0:8]
            for l in range(1, lag.shape[0]):
                total = total + lag[l : l + 1, cols] * room[at, l : l + 8, :]
            out[:, cols] = total


EDGE_UNITS = 8
INNER_UNITS = 64 - 2 * EDGE_UNITS


def run_inner(body):
    for j in range(INNER_UNITS):
        body(EDGE_UNITS + j, j)


def run_edge(body):
    for j in range(EDGE_UNITS):
        body(j, j)
    for j in range(EDGE_UNITS):
        body(64 - EDGE_UNITS + j, EDGE_UNITS + j)


def pass_call(kernel, cols, weights, half, halos, extra, held, new, edges, scratch, name):
    inputs = [cols, weights, half, *halos, *extra, *held]
    shapes = list(new) if not held else list(new)
    aliases = {3 + len(halos) + len(extra) + i: i for i in range(len(held))}
    sent = [jax.ShapeDtypeStruct((EDGE, 8, 2 * LANES), BF16)] * edges
    return pl.pallas_call(
        kernel,
        out_shape=tuple(shapes + sent),
        in_specs=[SSPEC] + [VSPEC] * (len(inputs) - 1),
        out_specs=(VSPEC,) * (len(shapes) + edges),
        scratch_shapes=scratch,
        input_output_aliases=aliases,
        compiler_params=pltpu.CompilerParams(vmem_limit_bytes=8 << 20),
        cost_estimate=pl.CostEstimate(
            flops=(1 << 30) if not held else (1 << 26), bytes_accessed=(16 << 20) if not held else (1 << 20), transcendentals=0
        ),
        name=name,
    )(inputs[0], *[in_vmem(x) for x in inputs[1:]])


def send_edges(half, lo, hi):
    lo[...] = half[0:EDGE]
    hi[...] = half[PART - EDGE : PART]


def inner_one(cols, weights, half, cheb, out_half):
    both, low = masks()

    def body(u, j):
        for d in range(2):
            m = 2 * u + d
            sums = group_product(m, cols, weights, half, both)
            finish_one((cheb, out_half), low, m, sums)

    run_inner(body)


def edge_one(cols, weights, half, below, above, cheb_in, half_in, cheb, out_half, lo, hi):
    both, low = masks()

    def body(u, j):
        for d in range(2):
            m = 2 * u + d
            sums = group_product(m, cols, weights, half, both, *((below, 0) if j < EDGE_UNITS else (above, 3)))
            finish_one((cheb, out_half), low, m, sums)

    run_edge(body)
    send_edges(out_half, lo, hi)


def inner_two(cols, weights, half, mixed, cheb, blend, out_half):
    both, low = masks()

    def body(u, j):
        for d in range(2):
            m = 2 * u + d
            sums = group_product(m, cols, weights, half, both)
            finish_two((mixed, cheb, blend, out_half), low, m, sums)

    run_inner(body)


def edge_two(cols, weights, half, below, above, mixed, cheb, blend_in, half_in, blend, out_half, lo, hi):
    both, low = masks()

    def body(u, j):
        for d in range(2):
            m = 2 * u + d
            sums = group_product(m, cols, weights, half, both, *((below, 0) if j < EDGE_UNITS else (above, 3)))
            finish_two((mixed, cheb, blend, out_half), low, m, sums)

    run_edge(body)
    send_edges(out_half, lo, hi)


def inner_three(cols, weights, half, blend, lag, out, room):
    both, low = masks()

    def body(u, j):
        filtered = []
        for d in range(2):
            m = 2 * u + d
            sums = group_product(m, cols, weights, half, both)
            filtered.append([blend[m, h] + 0.25 * sums[h] for h in range(2)])
        finish_three((lag, out, room, 4 * j), low, u, filtered)

    run_inner(body)


def edge_three(cols, weights, half, below, above, blend, lag, out_in, out, room):
    both, low = masks()

    def body(u, j):
        filtered = []
        for d in range(2):
            m = 2 * u + d
            sums = group_product(m, cols, weights, half, both, *((below, 0) if j < EDGE_UNITS else (above, 3)))
            filtered.append([blend[m, h] + 0.25 * sums[h] for h in range(2)])
        finish_three((lag, out, room, 4 * j), low, u, filtered)

    run_edge(body)


def passed_along(value, axis, by):
    peers = lax.axis_size(axis)
    return lax.ppermute(value, axis, [(i, (i + by) % peers) for i in range(peers)])


def edges_passed(first, last):
    return passed_along(last, "mesh", 1), passed_along(first, "mesh", -1)


def per_device(noise, lag, blocks, block_cols):
    cols = block_cols.T
    sent = noise.astype(BF16)
    following = passed_along(sent, "tm", -1)
    prev = passed_along(sent, "tm", 1)
    weights = repack(blocks)
    mixed, half, *sent = mix(noise, following, prev, lag, weights)

    field = pltpu.VMEM(mixed.shape, F32)
    packed = pltpu.VMEM(half.shape, BF16)
    result = pltpu.VMEM(noise.shape, F32)
    room = [pltpu.VMEM((4 * INNER_UNITS, 16, LANES), F32)]
    edge_room = [pltpu.VMEM((8 * EDGE_UNITS, 16, LANES), F32)]

    halos = edges_passed(*sent)
    held = pass_call(inner_one, cols, weights, half, (), (), (), (field, packed), 0, [], "inner_one")
    cheb, half, *sent = pass_call(
        edge_one, cols, weights, half, halos, (), held, (field, packed), 2, [], "edge_one"
    )
    halos = edges_passed(*sent)
    held = pass_call(inner_two, cols, weights, half, (), (mixed, cheb), (), (field, packed), 0, [], "inner_two")
    blend, half, *sent = pass_call(
        edge_two, cols, weights, half, halos, (mixed, cheb), held, (field, packed), 2, [], "edge_two"
    )
    halos = edges_passed(*sent)
    held = pass_call(inner_three, cols, weights, half, (), (blend, lag), (), (result,), 0, room, "inner_three")
    (out,) = pass_call(
        edge_three, cols, weights, half, halos, (blend, lag), held, (result,), 0, edge_room, "edge_three"
    )
    return out


def solution(mesh):
    placed = (P("tm", "mesh"), P(None, "mesh"), P("mesh", None, None, None), P("mesh", None))
    return jax.shard_map(
        per_device, mesh=mesh, in_specs=placed, out_specs=P("tm", "mesh"), check_vma=False
    )
```

```python
import functools

import jax
import jax.numpy as jnp
from jax import lax
from jax.experimental import pallas as pl
from jax.experimental.pallas import tpu as pltpu
from jax.sharding import PartitionSpec as P

LANES = 128
HALF = 64
EDGE = 16
PART = 512
F32 = jnp.float32
BF16 = jnp.bfloat16
VSPEC = pl.BlockSpec(memory_space=pltpu.VMEM)
SSPEC = pl.BlockSpec(memory_space=pltpu.SMEM)
ASPEC = pl.BlockSpec(memory_space=pl.ANY)


def in_hbm(x):
    return pltpu.with_memory_space_constraint(x, pltpu.HBM)


def in_vmem(x):
    return pltpu.with_memory_space_constraint(x, pltpu.VMEM)


def block_of(x, h, m):
    if x and h:
        return 384 + (m + (LANES - EDGE)) % LANES
    return 256 * x + 128 * h + m


def lane_bits(rows):
    return lax.broadcasted_iota(jnp.int32, (rows, LANES), 1)


def repack_kernel(src, out, held, stage, sems):
    ks, width, depth, blocks = src.shape
    deep = depth // 16
    units = ks * deep
    slots = held.shape[0]

    def place(u):
        return lax.div(u, deep), pl.multiple_of(lax.rem(u, deep) * 16, 16)

    def fetch(u):
        k, j = place(u)
        slot = lax.rem(u, slots)
        return pltpu.make_async_copy(src.at[k, :, pl.ds(j, 16), :], held.at[slot], sems.at[slot])

    lane = lax.broadcasted_iota(jnp.int32, (16, 2 * LANES), 1)
    masks = [(lane & (1 << s)) != 0 for s in range(7)]

    for u in range(slots - 1):
        fetch(u).start()

    def unit(u, carry):
        slot = lax.rem(u, slots)

        @pl.when(u + slots - 1 < units)
        def _():
            fetch(u + slots - 1).start()

        fetch(u).wait()
        k, j = place(u)
        row = pl.multiple_of(k * depth + j, 16)
        for r in range(8):
            vals = []
            for q in range(16):
                n = r + 8 * q
                at = 2 * LANES * (n // 64)
                v = held[slot, n % 64, :, at : at + 2 * LANES]
                if n:
                    far = (n + EDGE) % LANES if n >= 64 else n
                    right = v[:, LANES:]
                    right = pltpu.roll(right, far, 1) if far else right
                    v = jnp.concatenate([pltpu.roll(v[:, :LANES], n, 1), right], axis=1)
                vals.append(v)
            for s in range(4):
                vals = [jnp.where(masks[3 + s], vals[(q + (1 << s)) % 16], vals[q]) for q in range(16)]
            for q in range(16):
                stage[r + 8 * q] = vals[q]
        for c in range(16):
            vals = [stage[(8 * c + q) % 128] for q in range(15)]
            vals = [jnp.where(masks[2], vals[q + 4], vals[q]) for q in range(11)]
            vals = [jnp.where(masks[1], vals[q + 2], vals[q]) for q in range(9)]
            vals = [jnp.where(masks[0], vals[q + 1], vals[q]) for q in range(8)]
            for q in range(8):
                n = 8 * c + q
                out[(128 - n) % 128, pl.ds(row, 16), :] = vals[q]
        return carry

    def two_units(i, carry):
        return unit(2 * i + 1, unit(2 * i, carry))

    lax.fori_loop(0, units // 2, two_units, 0)


def repack(blocks):
    src = in_hbm(jnp.transpose(blocks, (1, 2, 3, 0)))
    ks, width, depth, count = src.shape
    slots = 4
    return pl.pallas_call(
        repack_kernel,
        out_shape=pltpu.VMEM((LANES, ks * depth, 2 * LANES), BF16),
        in_specs=[ASPEC],
        out_specs=VSPEC,
        scratch_shapes=[
            pltpu.VMEM((slots, width, 16, count), BF16),
            pltpu.VMEM((LANES, 16, 2 * LANES), BF16),
            pltpu.SemaphoreType.DMA((slots,)),
        ],
        compiler_params=pltpu.CompilerParams(vmem_limit_bytes=10 << 20),
        cost_estimate=pl.CostEstimate(flops=0, bytes_accessed=40 << 20, transcendentals=0),
        name="repack",
    )(src)


def swap_pair(low, first, second):
    return (
        jnp.where(low, first, pltpu.roll(second, HALF, 1)),
        jnp.where(low, pltpu.roll(first, HALF, 1), second),
    )


def doubled(low, tile):
    turned = pltpu.roll(tile, HALF, 1)
    return [
        jnp.concatenate([t[0:8], t[8:16]], axis=1).astype(BF16)
        for t in (jnp.where(low, tile, turned), jnp.where(low, turned, tile))
    ]


def mix_kernel(noise, following, prev, lag, weights, mixed, half, one, two, ext):
    lags = lag.shape[0]
    steps = noise.shape[0]
    low = lane_bits(2 * steps) < HALF

    def tile(t, slot):
        cols = pl.ds(pl.multiple_of(t * LANES, LANES), LANES)
        ext[slot, 0:8, :] = prev[:, cols].astype(F32)
        ext[slot, 8:16, :] = noise[:, cols]
        ext[slot, 16:24, :] = following[:, cols].astype(F32)
        total = lag[0:1, cols] * ext[slot, 8:24, :]
        for l in range(1, lags):
            total = total + lag[l : l + 1, cols] * ext[slot, 8 - l : 24 - l, :]
        return total

    def step(i, carry):
        for j in range(32):
            h, m = j % 2, 2 * (i * 16 + j // 2)
            b, c = block_of(0, h, m), block_of(1, h, m)
            first = tile(lax.div(b, 2), 2 * j)
            second = tile(lax.div(c, 2), 2 * j + 1)
            half[b], half[b + 1] = doubled(low, first)
            half[c], half[c + 1] = doubled(low, second)
            mixed[m, h], mixed[m + 1, h] = swap_pair(low, first, second)
        return carry

    lax.fori_loop(0, 4, step, 0)
    send_edges(masks()[0], half, one, two)


def mix(noise, following, prev, lag, weights):
    rows = 2 * noise.shape[0]
    tiles = noise.shape[1] // LANES
    return pl.pallas_call(
        mix_kernel,
        out_shape=(
            pltpu.VMEM((tiles // 2, 2, rows, LANES), F32),
            pltpu.VMEM((2 * tiles, 8, 2 * LANES), BF16),
            jax.ShapeDtypeStruct((EDGE // 2, 8, 2 * LANES), BF16),
            jax.ShapeDtypeStruct((EDGE // 2, 8, 2 * LANES), BF16),
        ),
        in_specs=[VSPEC] * 5,
        out_specs=(VSPEC,) * 4,
        scratch_shapes=[pltpu.VMEM((64, 24, LANES), F32)],
        compiler_params=pltpu.CompilerParams(vmem_limit_bytes=8 << 20),
        cost_estimate=pl.CostEstimate(flops=8 << 20, bytes_accessed=8 << 20, transcendentals=0),
        name="mix",
    )(*[in_vmem(x) for x in (noise, following, prev, lag, weights)])


def halo_block(even, odd, is_odd, at):
    pair = at >> 1
    held = jnp.where(is_odd, odd[pair], even[pair])
    turned = jnp.concatenate(
        [pltpu.roll(held[:, :LANES], HALF, 1), pltpu.roll(held[:, LANES:], HALF, 1)], axis=1
    )
    return jnp.where((at & 1) == 1, held, turned)


def group_product(m, cols, weights, half, low, halos=None):
    halos = halos or {}
    rows = []
    for j in range(4):
        b = block_of(j % 2, j // 2, m)
        picked = []
        for k in range(4):
            c = cols[k, b]
            value = half[c & (PART - 1)]
            if j in halos and k == 1:
                near = (c ^ cols[0, b]) < PART
                value = jnp.where(near, value, halo_block(*halos[j], c & (EDGE - 1)))
            picked.append(value)
        left = jnp.where(low, picked[0], picked[1])
        right = jnp.where(low, picked[2], picked[3])
        rows.append(jnp.concatenate([left[:, :LANES], right[:, :LANES]], axis=1))
        rows.append(jnp.concatenate([left[:, LANES:], right[:, LANES:]], axis=1))
    taken = jnp.concatenate(rows, axis=0)
    y = jnp.dot(taken, weights[m], preferred_element_type=F32)
    turned = ((lane_bits(16) - m) & HALF) == 0
    back = (LANES - m) & (LANES - 1)
    return [
        pltpu.roll(jnp.where(turned, y[r : r + 16, at : at + LANES], y[r + 16 : r + 32, at : at + LANES]), back, 1)
        for r, at in ((0, 0), (32, LANES))
    ]


def masks():
    both = (lax.broadcasted_iota(jnp.int32, (8, 2 * LANES), 1) & HALF) == 0
    return both, lane_bits(16) < HALF


def store_half(half, low, m, pairs):
    for h in range(2):
        half[block_of(0, h, m)], half[block_of(1, h, m)] = doubled(low, pairs[h])


def finish_one(refs, low, m, sums):
    cheb, half = refs
    for h in range(2):
        cheb[m, h] = sums[h]
    store_half(half, low, m, sums)


def finish_two(refs, low, m, sums):
    mixed, cheb, blend, half = refs
    second = []
    for h in range(2):
        at = mixed[m, h]
        second.append(2.0 * sums[h] - at)
        blend[m, h] = 0.75 * at + 0.375 * cheb[m, h] + 0.5 * sums[h]
    store_half(half, low, m, second)


def send_out(buffer, out, sems, units, at):
    copies = []
    for c in range(4):
        start = block_of(c % 2, c // 2, 2 * units[0]) * HALF
        cols = slice(start, start + (units[1] - units[0]) * LANES)
        copies.append(pltpu.make_async_copy(buffer.at[:, cols], out.at[:, cols], sems.at[4 * at + c]))
        copies[-1].start()
    return copies


def finish_three(refs, low, u, filtered):
    lag, out, room, slot = refs
    for h in range(2):
        natural = swap_pair(low, filtered[0][h], filtered[1][h])
        for d in range(2):
            at = slot + 2 * h + d
            room[at] = natural[d]
            cols = pl.ds(pl.multiple_of(block_of(d, h, 2 * u) * HALF, LANES), LANES)
            total = lag[0:1, cols] * natural[d][0:8]
            for l in range(1, lag.shape[0]):
                total = total + lag[l : l + 1, cols] * room[at, l : l + 8, :]
            out[:, cols] = total


EDGE_UNITS = 8
INNER_UNITS = 64 - EDGE_UNITS


def run_inner(body):
    for j in range(INNER_UNITS):
        body(EDGE_UNITS + j, j)


def run_edge(body):
    for j in range(EDGE_UNITS):
        body(j, j)


def pass_call(kernel, cols, weights, half, halos, extra, held, new, edges, scratch, name, space=VSPEC):
    inputs = [weights, half, *halos, *extra]
    aliases = {1 + len(inputs) + i: i for i in range(len(held))} if space is VSPEC else {}
    sent = [jax.ShapeDtypeStruct((EDGE // 2, 8, 2 * LANES), BF16)] * edges
    return pl.pallas_call(
        kernel,
        out_shape=(*new, *sent),
        in_specs=[SSPEC] + [VSPEC] * (len(inputs) + len(held)),
        out_specs=(space,) * len(new) + (VSPEC,) * edges,
        scratch_shapes=scratch,
        input_output_aliases=aliases,
        compiler_params=pltpu.CompilerParams(vmem_limit_bytes=8 << 20),
        cost_estimate=pl.CostEstimate(
            flops=(1 << 26) if held else (1 << 30), bytes_accessed=(1 << 20) if held else (16 << 20), transcendentals=0
        ),
        name=name,
    )(cols, *[in_vmem(x) for x in (*inputs, *held)])


def odd_slab():
    return lax.rem(lax.axis_index("tm"), 2)


def send_edges(both, half, one, two):
    odd = odd_slab()
    for to, start in ((one, (1 - odd) * (PART - EDGE)), (two, odd * (PART - EDGE))):
        for i in range(EDGE // 2):
            to[i] = jnp.where(both, half[start + 2 * i], half[start + 2 * i + 1])


def edge_rows(odd, first, second):
    return {0: (first, second, odd), 3: (second, first, odd)}


def inner_one(cols, weights, half, cheb, out_half):
    both, low = masks()

    def body(u, j):
        for d in range(2):
            m = 2 * u + d
            sums = group_product(m, cols, weights, half, both)
            finish_one((cheb, out_half), low, m, sums)

    run_inner(body)


def edge_one(cols, weights, half, first, second, cheb_in, half_in, cheb, out_half, one, two):
    both, low = masks()
    odd = odd_slab() == 1

    def body(u, j):
        for d in range(2):
            m = 2 * u + d
            sums = group_product(m, cols, weights, half, both, edge_rows(odd, first, second))
            finish_one((cheb, out_half), low, m, sums)

    run_edge(body)
    send_edges(both, out_half, one, two)


def inner_two(cols, weights, half, mixed, cheb, blend, out_half):
    both, low = masks()

    def body(u, j):
        for d in range(2):
            m = 2 * u + d
            sums = group_product(m, cols, weights, half, both)
            finish_two((mixed, cheb, blend, out_half), low, m, sums)

    run_inner(body)


def edge_two(cols, weights, half, first, second, mixed, cheb, blend_in, half_in, blend, out_half, one, two):
    both, low = masks()
    odd = odd_slab() == 1

    def body(u, j):
        for d in range(2):
            m = 2 * u + d
            sums = group_product(m, cols, weights, half, both, edge_rows(odd, first, second))
            finish_two((mixed, cheb, blend, out_half), low, m, sums)

    run_edge(body)
    send_edges(both, out_half, one, two)


def inner_three(cols, weights, half, blend, lag, out, room):
    both, low = masks()

    def body(u, j):
        filtered = []
        for d in range(2):
            m = 2 * u + d
            sums = group_product(m, cols, weights, half, both)
            filtered.append([blend[m, h] + 0.25 * sums[h] for h in range(2)])
        finish_three((lag, out, room, 4 * j), low, u, filtered)

    run_inner(body)


def edge_three(cols, weights, half, first, second, blend, lag, inner, out, room, buffer, sems):
    both, low = masks()
    odd = odd_slab() == 1

    copies = send_out(inner, out, sems, (EDGE_UNITS, 64), 0)

    def body(u, j):
        filtered = []
        for d in range(2):
            m = 2 * u + d
            sums = group_product(m, cols, weights, half, both, edge_rows(odd, first, second))
            filtered.append([blend[m, h] + 0.25 * sums[h] for h in range(2)])
        finish_three((lag, buffer, room, 4 * j), low, u, filtered)

    run_edge(body)
    copies += send_out(buffer, out, sems, (0, EDGE_UNITS), 1)
    for copy in copies:
        copy.wait()


def passed_along(value, axis, by):
    peers = lax.axis_size(axis)
    return lax.ppermute(value, axis, [(i, (i + by) % peers) for i in range(peers)])


def edges_passed(one, two):
    parts, slabs = lax.axis_size("mesh"), lax.axis_size("tm")
    ahead = []
    for t in range(slabs):
        for p in range(parts):
            q = p + (1 if t % 2 == 0 else -1)
            ahead.append((t * parts + p, t * parts + q if 0 <= q < parts else (t ^ 1) * parts + p))
    back = [(to, at) for at, to in ahead]
    return lax.ppermute(one, ("tm", "mesh"), ahead), lax.ppermute(two, ("tm", "mesh"), back)


def per_device(noise, lag, blocks, block_cols):
    cols = block_cols.T
    sent = noise.astype(BF16)
    following = passed_along(sent, "tm", -1)
    prev = passed_along(sent, "tm", 1)
    weights = repack(blocks)
    mixed, half, *sent = mix(noise, following, prev, lag, weights)

    field = pltpu.VMEM(mixed.shape, F32)
    packed = pltpu.VMEM(half.shape, BF16)
    result = pltpu.VMEM(noise.shape, F32)
    inner_room = [pltpu.VMEM((4 * INNER_UNITS, 16, LANES), F32)]
    edge_room = [
        pltpu.VMEM((4 * EDGE_UNITS, 16, LANES), F32),
        pltpu.VMEM(noise.shape, F32),
        pltpu.SemaphoreType.DMA((8,)),
    ]

    halos = edges_passed(*sent)
    held = pass_call(inner_one, cols, weights, half, (), (), (), (field, packed), 0, [], "inner_one")
    cheb, half, *sent = pass_call(
        edge_one, cols, weights, half, halos, (), held, (field, packed), 2, [], "edge_one"
    )
    halos = edges_passed(*sent)
    held = pass_call(inner_two, cols, weights, half, (), (mixed, cheb), (), (field, packed), 0, [], "inner_two")
    blend, half, *sent = pass_call(
        edge_two, cols, weights, half, halos, (mixed, cheb), held, (field, packed), 2, [], "edge_two"
    )
    halos = edges_passed(*sent)
    held = pass_call(inner_three, cols, weights, half, (), (blend, lag), (), (result,), 0, inner_room, "inner_three")
    (out,) = pass_call(
        edge_three, cols, weights, half, halos, (blend, lag), held, (pltpu.HBM(noise.shape, F32),), 0, edge_room, "edge_three", ASPEC
    )
    return out


def solution(mesh):
    placed = (P("tm", "mesh"), P(None, "mesh"), P("mesh", None, None, None), P("mesh", None))
    return jax.shard_map(
        per_device, mesh=mesh, in_specs=placed, out_specs=P("tm", "mesh"), check_vma=False
    )
```

```python
import functools

import jax
import jax.numpy as jnp
from jax import lax
from jax.experimental import pallas as pl
from jax.experimental.pallas import tpu as pltpu
from jax.sharding import PartitionSpec as P

LANES = 128
HALF = 64
EDGE = 16
PART = 512
F32 = jnp.float32
BF16 = jnp.bfloat16
VSPEC = pl.BlockSpec(memory_space=pltpu.VMEM)
SSPEC = pl.BlockSpec(memory_space=pltpu.SMEM)
ASPEC = pl.BlockSpec(memory_space=pl.ANY)


def in_hbm(x):
    return pltpu.with_memory_space_constraint(x, pltpu.HBM)


def in_vmem(x):
    return pltpu.with_memory_space_constraint(x, pltpu.VMEM)


def block_of(x, h, m):
    if x and h:
        return 384 + (m + (LANES - EDGE)) % LANES
    return 256 * x + 128 * h + m


def lane_bits(rows):
    return lax.broadcasted_iota(jnp.int32, (rows, LANES), 1)


def repack_kernel(src, out, held, stage, sems):
    ks, width, depth, blocks = src.shape
    tall = held.shape[2]
    deep = depth // tall
    units = ks * deep
    slots = held.shape[0]

    def place(u):
        return lax.div(u, deep), pl.multiple_of(lax.rem(u, deep) * tall, tall)

    parts = sems.shape[1]
    piece = width // parts

    class fetch:
        def __init__(self, u):
            k, j = place(u)
            slot = lax.rem(u, slots)
            self.copies = [
                pltpu.make_async_copy(
                    src.at[k, piece * i : piece * i + piece, pl.ds(j, tall), :],
                    held.at[slot, piece * i : piece * i + piece],
                    sems.at[slot, i],
                )
                for i in range(parts)
            ]

        def start(self):
            for copy in self.copies:
                copy.start()

        def wait(self):
            for copy in self.copies:
                copy.wait()

    lane = lax.broadcasted_iota(jnp.int32, (16, 2 * LANES), 1)
    masks = [(lane & (1 << s)) != 0 for s in range(7)]

    for u in range(slots - 1):
        fetch(u).start()

    def unit(u, carry):
        slot = lax.rem(u, slots)

        @pl.when(u + slots - 1 < units)
        def _():
            fetch(u + slots - 1).start()

        fetch(u).wait()
        k, j = place(u)
        for sub in range(tall // 16):
            row = pl.multiple_of(k * depth + j + 16 * sub, 16)
            for r in range(8):
                vals = []
                for q in range(16):
                    n = r + 8 * q
                    at = 2 * LANES * (n // 64)
                    v = held[slot, n % 64, 16 * sub : 16 * sub + 16, at : at + 2 * LANES]
                    if n:
                        far = (n + EDGE) % LANES if n >= 64 else n
                        right = v[:, LANES:]
                        right = pltpu.roll(right, far, 1) if far else right
                        v = jnp.concatenate([pltpu.roll(v[:, :LANES], n, 1), right], axis=1)
                    vals.append(v)
                for s in range(4):
                    vals = [jnp.where(masks[3 + s], vals[(q + (1 << s)) % 16], vals[q]) for q in range(16)]
                for q in range(16):
                    stage[r + 8 * q] = vals[q]
            for c in range(16):
                vals = [stage[(8 * c + q) % 128] for q in range(15)]
                vals = [jnp.where(masks[2], vals[q + 4], vals[q]) for q in range(11)]
                vals = [jnp.where(masks[1], vals[q + 2], vals[q]) for q in range(9)]
                vals = [jnp.where(masks[0], vals[q + 1], vals[q]) for q in range(8)]
                for q in range(8):
                    n = 8 * c + q
                    out[(128 - n) % 128, pl.ds(row, 16), :] = vals[q]
        return carry

    lax.fori_loop(0, units, unit, 0)


def repack(blocks):
    src = in_hbm(jnp.transpose(blocks, (1, 2, 3, 0)))
    ks, width, depth, count = src.shape
    slots = 3
    return pl.pallas_call(
        repack_kernel,
        out_shape=pltpu.VMEM((LANES, ks * depth, 2 * LANES), BF16),
        in_specs=[ASPEC],
        out_specs=VSPEC,
        scratch_shapes=[
            pltpu.VMEM((slots, width, 32, count), BF16),
            pltpu.VMEM((LANES, 16, 2 * LANES), BF16),
            pltpu.SemaphoreType.DMA((slots, 4)),
        ],
        compiler_params=pltpu.CompilerParams(vmem_limit_bytes=16 << 20),
        cost_estimate=pl.CostEstimate(flops=0, bytes_accessed=40 << 20, transcendentals=0),
        name="repack",
    )(src)


def swap_pair(low, first, second):
    return (
        jnp.where(low, first, pltpu.roll(second, HALF, 1)),
        jnp.where(low, pltpu.roll(first, HALF, 1), second),
    )


def doubled(low, tile):
    turned = pltpu.roll(tile, HALF, 1)
    return [
        jnp.concatenate([t[0:8], t[8:16]], axis=1).astype(BF16)
        for t in (jnp.where(low, tile, turned), jnp.where(low, turned, tile))
    ]


def mix_kernel(noise, following, prev, lag, weights, mixed, half, one, two, ext):
    lags = lag.shape[0]
    steps = noise.shape[0]
    low = lane_bits(2 * steps) < HALF

    def tile(t, slot):
        cols = slice(t * LANES, (t + 1) * LANES)
        ext[slot, 0:8, :] = prev[:, cols].astype(F32)
        ext[slot, 8:16, :] = noise[:, cols]
        ext[slot, 16:24, :] = following[:, cols].astype(F32)
        total = lag[0:1, cols] * ext[slot, 8:24, :]
        for l in range(1, lags):
            total = total + lag[l : l + 1, cols] * ext[slot, 8 - l : 24 - l, :]
        return total

    for g in range(noise.shape[1] // (2 * LANES)):
        h, m = g % 2, g - g % 2
        b, c = block_of(0, h, m), block_of(1, h, m)
        first = tile(b // 2, 2 * g)
        second = tile(c // 2, 2 * g + 1)
        half[b], half[b + 1] = doubled(low, first)
        half[c], half[c + 1] = doubled(low, second)
        mixed[m, h], mixed[m + 1, h] = swap_pair(low, first, second)
    send_edges(masks()[0], half, one, two)


def mix(noise, following, prev, lag, weights):
    rows = 2 * noise.shape[0]
    tiles = noise.shape[1] // LANES
    return pl.pallas_call(
        mix_kernel,
        out_shape=(
            pltpu.VMEM((tiles // 2, 2, rows, LANES), F32),
            pltpu.VMEM((2 * tiles, 8, 2 * LANES), BF16),
            jax.ShapeDtypeStruct((EDGE // 2, 8, 2 * LANES), BF16),
            jax.ShapeDtypeStruct((EDGE // 2, 8, 2 * LANES), BF16),
        ),
        in_specs=[VSPEC] * 5,
        out_specs=(VSPEC,) * 4,
        scratch_shapes=[pltpu.VMEM((tiles, 24, LANES), F32)],
        compiler_params=pltpu.CompilerParams(vmem_limit_bytes=8 << 20),
        cost_estimate=pl.CostEstimate(flops=8 << 20, bytes_accessed=8 << 20, transcendentals=0),
        name="mix",
    )(*[in_vmem(x) for x in (noise, following, prev, lag, weights)])


def halo_block(even, odd, is_odd, at):
    pair = at >> 1
    held = jnp.where(is_odd, odd[pair], even[pair])
    turned = jnp.concatenate(
        [pltpu.roll(held[:, :LANES], HALF, 1), pltpu.roll(held[:, LANES:], HALF, 1)], axis=1
    )
    return jnp.where((at & 1) == 1, held, turned)


def group_product(m, cols, weights, half, low, halos=None):
    halos = halos or {}
    rows = []
    for j in range(4):
        b = block_of(j % 2, j // 2, m)
        picked = []
        for k in range(4):
            c = cols[k, b]
            value = half[c & (PART - 1)]
            if j in halos and k == 1:
                near = (c ^ cols[0, b]) < PART
                value = jnp.where(near, value, halo_block(*halos[j], c & (EDGE - 1)))
            picked.append(value)
        left = jnp.where(low, picked[0], picked[1])
        right = jnp.where(low, picked[2], picked[3])
        rows.append(jnp.concatenate([left[:, :LANES], right[:, :LANES]], axis=1))
        rows.append(jnp.concatenate([left[:, LANES:], right[:, LANES:]], axis=1))
    taken = jnp.concatenate(rows, axis=0)
    y = jnp.dot(taken, weights[m], preferred_element_type=F32)
    turned = ((lane_bits(16) - m) & HALF) == 0
    back = (LANES - m) & (LANES - 1)
    return [
        pltpu.roll(jnp.where(turned, y[r : r + 16, at : at + LANES], y[r + 16 : r + 32, at : at + LANES]), back, 1)
        for r, at in ((0, 0), (32, LANES))
    ]


def masks():
    both = (lax.broadcasted_iota(jnp.int32, (8, 2 * LANES), 1) & HALF) == 0
    return both, lane_bits(16) < HALF


def store_half(half, low, m, pairs):
    for h in range(2):
        half[block_of(0, h, m)], half[block_of(1, h, m)] = doubled(low, pairs[h])


def finish_one(refs, low, m, sums):
    cheb, half = refs
    for h in range(2):
        cheb[m, h] = sums[h]
    store_half(half, low, m, sums)


def finish_two(refs, low, m, sums):
    mixed, cheb, blend, half = refs
    second = []
    for h in range(2):
        at = mixed[m, h]
        second.append(2.0 * sums[h] - at)
        blend[m, h] = 0.75 * at + 0.375 * cheb[m, h] + 0.5 * sums[h]
    store_half(half, low, m, second)


def send_out(buffer, out, sems, units, at):
    copies = []
    for c in range(4):
        start = block_of(c % 2, c // 2, 2 * units[0]) * HALF
        cols = slice(start, start + (units[1] - units[0]) * LANES)
        copies.append(pltpu.make_async_copy(buffer.at[:, cols], out.at[:, cols], sems.at[4 * at + c]))
        copies[-1].start()
    return copies


def finish_three(refs, low, u, filtered):
    lag, out, room, slot = refs
    for h in range(2):
        natural = swap_pair(low, filtered[0][h], filtered[1][h])
        for d in range(2):
            at = slot + 2 * h + d
            room[at] = natural[d]
            cols = pl.ds(pl.multiple_of(block_of(d, h, 2 * u) * HALF, LANES), LANES)
            total = lag[0:1, cols] * natural[d][0:8]
            for l in range(1, lag.shape[0]):
                total = total + lag[l : l + 1, cols] * room[at, l : l + 8, :]
            out[:, cols] = total


EDGE_UNITS = 8
INNER_UNITS = 64 - EDGE_UNITS


def run_inner(body):
    for j in range(INNER_UNITS):
        body(EDGE_UNITS + j, j)


def run_edge(body):
    for j in range(EDGE_UNITS):
        body(j, j)


def pass_call(kernel, cols, weights, half, halos, extra, held, new, edges, scratch, name, space=VSPEC):
    inputs = [weights, half, *halos, *extra]
    aliases = {1 + len(inputs) + i: i for i in range(len(held))} if space is VSPEC else {}
    sent = [jax.ShapeDtypeStruct((EDGE // 2, 8, 2 * LANES), BF16)] * edges
    return pl.pallas_call(
        kernel,
        out_shape=(*new, *sent),
        in_specs=[SSPEC] + [VSPEC] * (len(inputs) + len(held)),
        out_specs=(space,) * len(new) + (VSPEC,) * edges,
        scratch_shapes=scratch,
        input_output_aliases=aliases,
        compiler_params=pltpu.CompilerParams(vmem_limit_bytes=8 << 20),
        cost_estimate=pl.CostEstimate(
            flops=(1 << 26) if held else (1 << 30), bytes_accessed=(1 << 20) if held else (16 << 20), transcendentals=0
        ),
        name=name,
    )(cols, *[in_vmem(x) for x in (*inputs, *held)])


def odd_part():
    return lax.rem(lax.axis_index("mesh"), 2)


def send_edges(both, half, one, two):
    odd = odd_part()
    for to, start in ((one, (1 - odd) * (PART - EDGE)), (two, odd * (PART - EDGE))):
        for i in range(EDGE // 2):
            to[i] = jnp.where(both, half[start + 2 * i], half[start + 2 * i + 1])


def edge_rows(odd, first, second):
    return {0: (second, first, odd), 3: (first, second, odd)}


def inner_one(cols, weights, half, cheb, out_half):
    both, low = masks()

    def body(u, j):
        for d in range(2):
            m = 2 * u + d
            sums = group_product(m, cols, weights, half, both)
            finish_one((cheb, out_half), low, m, sums)

    run_inner(body)


def edge_one(cols, weights, half, first, second, cheb_in, half_in, cheb, out_half, one, two):
    both, low = masks()
    odd = odd_part() == 1

    def body(u, j):
        for d in range(2):
            m = 2 * u + d
            sums = group_product(m, cols, weights, half, both, edge_rows(odd, first, second))
            finish_one((cheb, out_half), low, m, sums)

    run_edge(body)
    send_edges(both, out_half, one, two)


def inner_two(cols, weights, half, mixed, cheb, blend, out_half):
    both, low = masks()

    def body(u, j):
        for d in range(2):
            m = 2 * u + d
            sums = group_product(m, cols, weights, half, both)
            finish_two((mixed, cheb, blend, out_half), low, m, sums)

    run_inner(body)


def edge_two(cols, weights, half, first, second, mixed, cheb, blend_in, half_in, blend, out_half, one, two):
    both, low = masks()
    odd = odd_part() == 1

    def body(u, j):
        for d in range(2):
            m = 2 * u + d
            sums = group_product(m, cols, weights, half, both, edge_rows(odd, first, second))
            finish_two((mixed, cheb, blend, out_half), low, m, sums)

    run_edge(body)
    send_edges(both, out_half, one, two)


def inner_three(cols, weights, half, blend, lag, out, room):
    both, low = masks()

    def body(u, j):
        filtered = []
        for d in range(2):
            m = 2 * u + d
            sums = group_product(m, cols, weights, half, both)
            filtered.append([blend[m, h] + 0.25 * sums[h] for h in range(2)])
        finish_three((lag, out, room, 4 * j), low, u, filtered)

    run_inner(body)


def edge_three(cols, weights, half, first, second, blend, lag, inner, out, room, buffer, sems):
    both, low = masks()
    odd = odd_part() == 1

    copies = send_out(inner, out, sems, (EDGE_UNITS, 64), 0)

    def body(u, j):
        filtered = []
        for d in range(2):
            m = 2 * u + d
            sums = group_product(m, cols, weights, half, both, edge_rows(odd, first, second))
            filtered.append([blend[m, h] + 0.25 * sums[h] for h in range(2)])
        finish_three((lag, buffer, room, 4 * j), low, u, filtered)

    run_edge(body)
    copies += send_out(buffer, out, sems, (0, EDGE_UNITS), 1)
    for copy in copies:
        copy.wait()


def passed_along(value, axis, by):
    peers = lax.axis_size(axis)
    return lax.ppermute(value, axis, [(i, (i + by) % peers) for i in range(peers)])


def edges_passed(one, two):
    parts, slabs = lax.axis_size("mesh"), lax.axis_size("tm")
    near, far = [], []
    for t in range(slabs):
        for p in range(parts):
            for pairs, q in ((near, p ^ 1), (far, ((p + 1) ^ 1) - 1)):
                pairs.append((t * parts + p, t * parts + q if 0 <= q < parts else (t ^ 1) * parts + p))
    return lax.ppermute(one, ("tm", "mesh"), near), lax.ppermute(two, ("tm", "mesh"), far)


def per_device(noise, lag, blocks, block_cols):
    cols = block_cols.T
    sent = noise.astype(BF16)
    following = passed_along(sent, "tm", -1)
    prev = passed_along(sent, "tm", 1)
    weights = repack(blocks)
    mixed, half, *sent = mix(noise, following, prev, lag, weights)

    field = pltpu.VMEM(mixed.shape, F32)
    packed = pltpu.VMEM(half.shape, BF16)
    result = pltpu.VMEM(noise.shape, F32)
    inner_room = [pltpu.VMEM((4 * INNER_UNITS, 16, LANES), F32)]
    edge_room = [
        pltpu.VMEM((4 * EDGE_UNITS, 16, LANES), F32),
        pltpu.VMEM(noise.shape, F32),
        pltpu.SemaphoreType.DMA((8,)),
    ]

    halos = edges_passed(*sent)
    held = pass_call(inner_one, cols, weights, half, (), (), (), (field, packed), 0, [], "inner_one")
    cheb, half, *sent = pass_call(
        edge_one, cols, weights, half, halos, (), held, (field, packed), 2, [], "edge_one"
    )
    halos = edges_passed(*sent)
    held = pass_call(inner_two, cols, weights, half, (), (mixed, cheb), (), (field, packed), 0, [], "inner_two")
    blend, half, *sent = pass_call(
        edge_two, cols, weights, half, halos, (mixed, cheb), held, (field, packed), 2, [], "edge_two"
    )
    halos = edges_passed(*sent)
    held = pass_call(inner_three, cols, weights, half, (), (blend, lag), (), (result,), 0, inner_room, "inner_three")
    (out,) = pass_call(
        edge_three, cols, weights, half, halos, (blend, lag), held, (pltpu.HBM(noise.shape, F32),), 0, edge_room, "edge_three", ASPEC
    )
    return out


def solution(mesh):
    placed = (P("tm", "mesh"), P(None, "mesh"), P("mesh", None, None, None), P("mesh", None))
    return jax.shard_map(
        per_device, mesh=mesh, in_specs=placed, out_specs=P("tm", "mesh"), check_vma=False
    )
```

```python
import functools

import jax
import jax.numpy as jnp
from jax import lax
from jax.experimental import pallas as pl
from jax.experimental.pallas import tpu as pltpu
from jax.sharding import PartitionSpec as P

LANES = 128
HALF = 64
EDGE = 16
PART = 512
F32 = jnp.float32
BF16 = jnp.bfloat16
VSPEC = pl.BlockSpec(memory_space=pltpu.VMEM)
SSPEC = pl.BlockSpec(memory_space=pltpu.SMEM)
ASPEC = pl.BlockSpec(memory_space=pl.ANY)


def in_hbm(x):
    return pltpu.with_memory_space_constraint(x, pltpu.HBM)


def in_vmem(x):
    return pltpu.with_memory_space_constraint(x, pltpu.VMEM)


def block_of(x, h, m):
    if x and h:
        return 384 + (m + (LANES - EDGE)) % LANES
    return 256 * x + 128 * h + m


def lane_bits(rows):
    return lax.broadcasted_iota(jnp.int32, (rows, LANES), 1)


def repack_kernel(src, out, held, stage, sems):
    ks, width, depth, blocks = src.shape
    tall = held.shape[2]
    deep = depth // tall
    units = ks * deep
    slots = held.shape[0]

    def place(u):
        return lax.div(u, deep), pl.multiple_of(lax.rem(u, deep) * tall, tall)

    parts = sems.shape[1]
    piece = width // parts

    class fetch:
        def __init__(self, u):
            k, j = place(u)
            slot = lax.rem(u, slots)
            self.copies = [
                pltpu.make_async_copy(
                    src.at[k, piece * i : piece * i + piece, pl.ds(j, tall), :],
                    held.at[slot, piece * i : piece * i + piece],
                    sems.at[slot, i],
                )
                for i in range(parts)
            ]

        def start(self):
            for copy in self.copies:
                copy.start()

        def wait(self):
            for copy in self.copies:
                copy.wait()

    lane = lax.broadcasted_iota(jnp.int32, (16, 2 * LANES), 1)
    masks = [(lane & (1 << s)) != 0 for s in range(7)]

    for u in range(slots - 1):
        fetch(u).start()

    def unit(u, carry):
        slot = lax.rem(u, slots)

        @pl.when(u + slots - 1 < units)
        def _():
            fetch(u + slots - 1).start()

        fetch(u).wait()
        k, j = place(u)
        for sub in range(tall // 16):
            row = pl.multiple_of(k * depth + j + 16 * sub, 16)
            for r in range(8):
                vals = []
                for q in range(16):
                    n = r + 8 * q
                    at = 2 * LANES * (n // 64)
                    v = held[slot, n % 64, 16 * sub : 16 * sub + 16, at : at + 2 * LANES]
                    if n:
                        far = (n + EDGE) % LANES if n >= 64 else n
                        right = v[:, LANES:]
                        right = pltpu.roll(right, far, 1) if far else right
                        v = jnp.concatenate([pltpu.roll(v[:, :LANES], n, 1), right], axis=1)
                    vals.append(v)
                for s in range(4):
                    vals = [jnp.where(masks[3 + s], vals[(q + (1 << s)) % 16], vals[q]) for q in range(16)]
                for q in range(16):
                    stage[r + 8 * q] = vals[q]
            for c in range(16):
                vals = [stage[(8 * c + q) % 128] for q in range(15)]
                vals = [jnp.where(masks[2], vals[q + 4], vals[q]) for q in range(11)]
                vals = [jnp.where(masks[1], vals[q + 2], vals[q]) for q in range(9)]
                vals = [jnp.where(masks[0], vals[q + 1], vals[q]) for q in range(8)]
                for q in range(8):
                    n = 8 * c + q
                    out[(128 - n) % 128, pl.ds(row, 16), :] = vals[q]
        return carry

    lax.fori_loop(0, units, unit, 0)


def repack(blocks):
    src = in_hbm(jnp.transpose(blocks, (1, 2, 3, 0)))
    ks, width, depth, count = src.shape
    slots = 3
    return pl.pallas_call(
        repack_kernel,
        out_shape=pltpu.VMEM((LANES, ks * depth, 2 * LANES), BF16),
        in_specs=[ASPEC],
        out_specs=VSPEC,
        scratch_shapes=[
            pltpu.VMEM((slots, width, 32, count), BF16),
            pltpu.VMEM((LANES, 16, 2 * LANES), BF16),
            pltpu.SemaphoreType.DMA((slots, 4)),
        ],
        compiler_params=pltpu.CompilerParams(vmem_limit_bytes=16 << 20),
        cost_estimate=pl.CostEstimate(flops=0, bytes_accessed=40 << 20, transcendentals=0),
        name="repack",
    )(src)


def cast_kernel(noise, sent, slab, sems):
    pieces = sems.shape[0]
    width = noise.shape[1] // pieces
    copies = []
    for i in range(pieces):
        cols = slice(i * width, (i + 1) * width)
        copies.append(pltpu.make_async_copy(noise.at[:, cols], slab.at[:, cols], sems.at[i]))
        copies[-1].start()
    for i in range(pieces):
        copies[i].wait()
        cols = slice(i * width, (i + 1) * width)
        sent[:, cols] = slab[:, cols].astype(BF16)


def cast(noise):
    return pl.pallas_call(
        cast_kernel,
        out_shape=(pltpu.VMEM(noise.shape, BF16), pltpu.VMEM(noise.shape, F32)),
        in_specs=[ASPEC],
        out_specs=(VSPEC, VSPEC),
        scratch_shapes=[pltpu.SemaphoreType.DMA((4,))],
        compiler_params=pltpu.CompilerParams(vmem_limit_bytes=4 << 20),
        cost_estimate=pl.CostEstimate(flops=0, bytes_accessed=1 << 20, transcendentals=0),
        name="cast",
    )(in_hbm(noise))


def swap_pair(low, first, second):
    return (
        jnp.where(low, first, pltpu.roll(second, HALF, 1)),
        jnp.where(low, pltpu.roll(first, HALF, 1), second),
    )


def doubled(low, tile):
    turned = pltpu.roll(tile, HALF, 1)
    return [
        jnp.concatenate([t[0:8], t[8:16]], axis=1).astype(BF16)
        for t in (jnp.where(low, tile, turned), jnp.where(low, turned, tile))
    ]


def mix_kernel(noise, following, prev, lag, weights, mixed, half, one, two, ext):
    lags = lag.shape[0]
    steps = noise.shape[0]
    low = lane_bits(2 * steps) < HALF

    def tile(t, slot):
        cols = slice(t * LANES, (t + 1) * LANES)
        ext[slot, 0:8, :] = prev[:, cols].astype(F32)
        ext[slot, 8:16, :] = noise[:, cols]
        ext[slot, 16:24, :] = following[:, cols].astype(F32)
        total = lag[0:1, cols] * ext[slot, 8:24, :]
        for l in range(1, lags):
            total = total + lag[l : l + 1, cols] * ext[slot, 8 - l : 24 - l, :]
        return total

    for g in range(noise.shape[1] // (2 * LANES)):
        h, m = g % 2, g - g % 2
        b, c = block_of(0, h, m), block_of(1, h, m)
        first = tile(b // 2, 2 * g)
        second = tile(c // 2, 2 * g + 1)
        half[b], half[b + 1] = doubled(low, first)
        half[c], half[c + 1] = doubled(low, second)
        mixed[m, h], mixed[m + 1, h] = swap_pair(low, first, second)
    send_edges(masks()[0], half, one, two)


def mix(noise, following, prev, lag, weights):
    rows = 2 * noise.shape[0]
    tiles = noise.shape[1] // LANES
    return pl.pallas_call(
        mix_kernel,
        out_shape=(
            pltpu.VMEM((tiles // 2, 2, rows, LANES), F32),
            pltpu.VMEM((2 * tiles, 8, 2 * LANES), BF16),
            jax.ShapeDtypeStruct((EDGE // 2, 8, 2 * LANES), BF16),
            jax.ShapeDtypeStruct((EDGE // 2, 8, 2 * LANES), BF16),
        ),
        in_specs=[VSPEC] * 5,
        out_specs=(VSPEC,) * 4,
        scratch_shapes=[pltpu.VMEM((tiles, 24, LANES), F32)],
        compiler_params=pltpu.CompilerParams(vmem_limit_bytes=8 << 20),
        cost_estimate=pl.CostEstimate(flops=8 << 20, bytes_accessed=8 << 20, transcendentals=0),
        name="mix",
    )(*[in_vmem(x) for x in (noise, following, prev, lag, weights)])


def halo_block(even, odd, is_odd, at):
    pair = at >> 1
    held = jnp.where(is_odd, odd[pair], even[pair])
    turned = jnp.concatenate(
        [pltpu.roll(held[:, :LANES], HALF, 1), pltpu.roll(held[:, LANES:], HALF, 1)], axis=1
    )
    return jnp.where((at & 1) == 1, held, turned)


def group_product(m, cols, weights, half, low, halos=None):
    halos = halos or {}
    rows = []
    for j in range(4):
        b = block_of(j % 2, j // 2, m)
        picked = []
        for k in range(4):
            c = cols[k, b]
            value = half[c & (PART - 1)]
            if j in halos and k == 1:
                near = (c ^ cols[0, b]) < PART
                value = jnp.where(near, value, halo_block(*halos[j], c & (EDGE - 1)))
            picked.append(value)
        left = jnp.where(low, picked[0], picked[1])
        right = jnp.where(low, picked[2], picked[3])
        rows.append(jnp.concatenate([left[:, :LANES], right[:, :LANES]], axis=1))
        rows.append(jnp.concatenate([left[:, LANES:], right[:, LANES:]], axis=1))
    taken = jnp.concatenate(rows, axis=0)
    y = jnp.dot(taken, weights[m], preferred_element_type=F32)
    turned = ((lane_bits(16) - m) & HALF) == 0
    back = (LANES - m) & (LANES - 1)
    return [
        pltpu.roll(jnp.where(turned, y[r : r + 16, at : at + LANES], y[r + 16 : r + 32, at : at + LANES]), back, 1)
        for r, at in ((0, 0), (32, LANES))
    ]


def masks():
    both = (lax.broadcasted_iota(jnp.int32, (8, 2 * LANES), 1) & HALF) == 0
    return both, lane_bits(16) < HALF


def store_half(half, low, m, pairs):
    for h in range(2):
        half[block_of(0, h, m)], half[block_of(1, h, m)] = doubled(low, pairs[h])


def finish_one(refs, low, m, sums):
    cheb, half = refs
    for h in range(2):
        cheb[m, h] = sums[h]
    store_half(half, low, m, sums)


def finish_two(refs, low, m, sums):
    mixed, cheb, blend, half = refs
    second = []
    for h in range(2):
        at = mixed[m, h]
        second.append(2.0 * sums[h] - at)
        blend[m, h] = 0.75 * at + 0.375 * cheb[m, h] + 0.5 * sums[h]
    store_half(half, low, m, second)


def send_out(buffer, out, sems, units, at):
    copies = []
    for c in range(4):
        start = block_of(c % 2, c // 2, 2 * units[0]) * HALF
        cols = slice(start, start + (units[1] - units[0]) * LANES)
        copies.append(pltpu.make_async_copy(buffer.at[:, cols], out.at[:, cols], sems.at[4 * at + c]))
        copies[-1].start()
    return copies


def finish_three(refs, low, u, filtered):
    lag, out, room, slot = refs
    for h in range(2):
        natural = swap_pair(low, filtered[0][h], filtered[1][h])
        for d in range(2):
            at = slot + 2 * h + d
            room[at] = natural[d]
            cols = pl.ds(pl.multiple_of(block_of(d, h, 2 * u) * HALF, LANES), LANES)
            total = lag[0:1, cols] * natural[d][0:8]
            for l in range(1, lag.shape[0]):
                total = total + lag[l : l + 1, cols] * room[at, l : l + 8, :]
            out[:, cols] = total


EDGE_UNITS = 8
INNER_UNITS = 64 - EDGE_UNITS


def run_inner(body):
    for j in range(INNER_UNITS):
        body(EDGE_UNITS + j, j)


def run_edge(body):
    for j in range(EDGE_UNITS):
        body(j, j)


def pass_call(kernel, cols, weights, half, halos, extra, held, new, edges, scratch, name, space=VSPEC):
    inputs = [weights, half, *halos, *extra]
    aliases = {1 + len(inputs) + i: i for i in range(len(held))} if space is VSPEC else {}
    sent = [jax.ShapeDtypeStruct((EDGE // 2, 8, 2 * LANES), BF16)] * edges
    return pl.pallas_call(
        kernel,
        out_shape=(*new, *sent),
        in_specs=[SSPEC] + [VSPEC] * (len(inputs) + len(held)),
        out_specs=(space,) * len(new) + (VSPEC,) * edges,
        scratch_shapes=scratch,
        input_output_aliases=aliases,
        compiler_params=pltpu.CompilerParams(vmem_limit_bytes=8 << 20),
        cost_estimate=pl.CostEstimate(
            flops=(1 << 26) if held else (1 << 30), bytes_accessed=(1 << 20) if held else (16 << 20), transcendentals=0
        ),
        name=name,
    )(cols, *[in_vmem(x) for x in (*inputs, *held)])


def odd_part():
    return lax.rem(lax.axis_index("mesh"), 2)


def send_edges(both, half, one, two):
    odd = odd_part()
    for to, start in ((one, (1 - odd) * (PART - EDGE)), (two, odd * (PART - EDGE))):
        for i in range(EDGE // 2):
            to[i] = jnp.where(both, half[start + 2 * i], half[start + 2 * i + 1])


def edge_rows(odd, first, second):
    return {0: (second, first, odd), 3: (first, second, odd)}


def inner_one(cols, weights, half, cheb, out_half):
    both, low = masks()

    def body(u, j):
        for d in range(2):
            m = 2 * u + d
            sums = group_product(m, cols, weights, half, both)
            finish_one((cheb, out_half), low, m, sums)

    run_inner(body)


def edge_one(cols, weights, half, first, second, cheb_in, half_in, cheb, out_half, one, two):
    both, low = masks()
    odd = odd_part() == 1

    def body(u, j):
        for d in range(2):
            m = 2 * u + d
            sums = group_product(m, cols, weights, half, both, edge_rows(odd, first, second))
            finish_one((cheb, out_half), low, m, sums)

    run_edge(body)
    send_edges(both, out_half, one, two)


def inner_two(cols, weights, half, mixed, cheb, blend, out_half):
    both, low = masks()

    def body(u, j):
        for d in range(2):
            m = 2 * u + d
            sums = group_product(m, cols, weights, half, both)
            finish_two((mixed, cheb, blend, out_half), low, m, sums)

    run_inner(body)


def edge_two(cols, weights, half, first, second, mixed, cheb, blend_in, half_in, blend, out_half, one, two):
    both, low = masks()
    odd = odd_part() == 1

    def body(u, j):
        for d in range(2):
            m = 2 * u + d
            sums = group_product(m, cols, weights, half, both, edge_rows(odd, first, second))
            finish_two((mixed, cheb, blend, out_half), low, m, sums)

    run_edge(body)
    send_edges(both, out_half, one, two)


def inner_three(cols, weights, half, blend, lag, out, room):
    both, low = masks()

    def body(u, j):
        filtered = []
        for d in range(2):
            m = 2 * u + d
            sums = group_product(m, cols, weights, half, both)
            filtered.append([blend[m, h] + 0.25 * sums[h] for h in range(2)])
        finish_three((lag, out, room, 4 * j), low, u, filtered)

    run_inner(body)


def edge_three(cols, weights, half, first, second, blend, lag, inner, out, room, buffer, sems):
    both, low = masks()
    odd = odd_part() == 1

    copies = send_out(inner, out, sems, (EDGE_UNITS, 64), 0)

    def body(u, j):
        filtered = []
        for d in range(2):
            m = 2 * u + d
            sums = group_product(m, cols, weights, half, both, edge_rows(odd, first, second))
            filtered.append([blend[m, h] + 0.25 * sums[h] for h in range(2)])
        finish_three((lag, buffer, room, 4 * j), low, u, filtered)

    run_edge(body)
    copies += send_out(buffer, out, sems, (0, EDGE_UNITS), 1)
    for copy in copies:
        copy.wait()


def passed_along(value, axis, by):
    peers = lax.axis_size(axis)
    return lax.ppermute(value, axis, [(i, (i + by) % peers) for i in range(peers)])


def edges_passed(one, two):
    parts, slabs = lax.axis_size("mesh"), lax.axis_size("tm")
    near, far = [], []
    for t in range(slabs):
        for p in range(parts):
            for pairs, q in ((near, p ^ 1), (far, ((p + 1) ^ 1) - 1)):
                pairs.append((t * parts + p, t * parts + q if 0 <= q < parts else (t ^ 1) * parts + p))
    return lax.ppermute(one, ("tm", "mesh"), near), lax.ppermute(two, ("tm", "mesh"), far)


def per_device(noise, lag, blocks, block_cols):
    cols = block_cols.T
    sent, slab = cast(noise)
    following = passed_along(sent, "tm", -1)
    prev = passed_along(sent, "tm", 1)
    weights = repack(blocks)
    mixed, half, *sent = mix(slab, following, prev, lag, weights)

    field = pltpu.VMEM(mixed.shape, F32)
    packed = pltpu.VMEM(half.shape, BF16)
    result = pltpu.VMEM(noise.shape, F32)
    inner_room = [pltpu.VMEM((4 * INNER_UNITS, 16, LANES), F32)]
    edge_room = [
        pltpu.VMEM((4 * EDGE_UNITS, 16, LANES), F32),
        pltpu.VMEM(noise.shape, F32),
        pltpu.SemaphoreType.DMA((8,)),
    ]

    halos = edges_passed(*sent)
    held = pass_call(inner_one, cols, weights, half, (), (), (), (field, packed), 0, [], "inner_one")
    cheb, half, *sent = pass_call(
        edge_one, cols, weights, half, halos, (), held, (field, packed), 2, [], "edge_one"
    )
    halos = edges_passed(*sent)
    held = pass_call(inner_two, cols, weights, half, (), (mixed, cheb), (), (field, packed), 0, [], "inner_two")
    blend, half, *sent = pass_call(
        edge_two, cols, weights, half, halos, (mixed, cheb), held, (field, packed), 2, [], "edge_two"
    )
    halos = edges_passed(*sent)
    held = pass_call(inner_three, cols, weights, half, (), (blend, lag), (), (result,), 0, inner_room, "inner_three")
    (out,) = pass_call(
        edge_three, cols, weights, half, halos, (blend, lag), held, (pltpu.HBM(noise.shape, F32),), 0, edge_room, "edge_three", ASPEC
    )
    return out


def solution(mesh):
    placed = (P("tm", "mesh"), P(None, "mesh"), P("mesh", None, None, None), P("mesh", None))
    return jax.shard_map(
        per_device, mesh=mesh, in_specs=placed, out_specs=P("tm", "mesh"), check_vma=False
    )
```

```python
import functools

import jax
import jax.numpy as jnp
from jax import lax
from jax.experimental import pallas as pl
from jax.experimental.pallas import tpu as pltpu
from jax.sharding import PartitionSpec as P

LANES = 128
HALF = 64
EDGE = 16
PART = 512
F32 = jnp.float32
BF16 = jnp.bfloat16
VSPEC = pl.BlockSpec(memory_space=pltpu.VMEM)
SSPEC = pl.BlockSpec(memory_space=pltpu.SMEM)
ASPEC = pl.BlockSpec(memory_space=pl.ANY)


def in_hbm(x):
    return pltpu.with_memory_space_constraint(x, pltpu.HBM)


def in_vmem(x):
    return pltpu.with_memory_space_constraint(x, pltpu.VMEM)


def block_of(x, h, m):
    if x and h:
        return 384 + (m + (LANES - EDGE)) % LANES
    return 256 * x + 128 * h + m


def lane_bits(rows):
    return lax.broadcasted_iota(jnp.int32, (rows, LANES), 1)


def repack_kernel(src, out, held, stage, sems):
    ks, width, depth, blocks = src.shape
    tall = held.shape[2]
    deep = depth // tall
    units = ks * deep
    slots = held.shape[0]

    def place(u):
        return lax.div(u, deep), pl.multiple_of(lax.rem(u, deep) * tall, tall)

    parts = sems.shape[1]
    piece = width // parts

    class fetch:
        def __init__(self, u):
            k, j = place(u)
            slot = lax.rem(u, slots)
            self.copies = [
                pltpu.make_async_copy(
                    src.at[k, piece * i : piece * i + piece, pl.ds(j, tall), :],
                    held.at[slot, piece * i : piece * i + piece],
                    sems.at[slot, i],
                )
                for i in range(parts)
            ]

        def start(self):
            for copy in self.copies:
                copy.start()

        def wait(self):
            for copy in self.copies:
                copy.wait()

    lane = lax.broadcasted_iota(jnp.int32, (16, 2 * LANES), 1)
    masks = [(lane & (1 << s)) != 0 for s in range(7)]

    for u in range(slots - 1):
        fetch(u).start()

    def unit(u, carry):
        slot = lax.rem(u, slots)

        @pl.when(u + slots - 1 < units)
        def _():
            fetch(u + slots - 1).start()

        fetch(u).wait()
        k, j = place(u)
        for sub in range(tall // 16):
            row = pl.multiple_of(k * depth + j + 16 * sub, 16)
            for r in range(8):
                vals = []
                for q in range(16):
                    n = r + 8 * q
                    at = 2 * LANES * (n // 64)
                    v = held[slot, n % 64, 16 * sub : 16 * sub + 16, at : at + 2 * LANES]
                    if n:
                        far = (n + EDGE) % LANES if n >= 64 else n
                        right = v[:, LANES:]
                        right = pltpu.roll(right, far, 1) if far else right
                        v = jnp.concatenate([pltpu.roll(v[:, :LANES], n, 1), right], axis=1)
                    vals.append(v)
                for s in range(4):
                    vals = [jnp.where(masks[3 + s], vals[(q + (1 << s)) % 16], vals[q]) for q in range(16)]
                for q in range(16):
                    stage[r + 8 * q] = vals[q]
            for c in range(16):
                vals = [stage[(8 * c + q) % 128] for q in range(15)]
                vals = [jnp.where(masks[2], vals[q + 4], vals[q]) for q in range(11)]
                vals = [jnp.where(masks[1], vals[q + 2], vals[q]) for q in range(9)]
                vals = [jnp.where(masks[0], vals[q + 1], vals[q]) for q in range(8)]
                for q in range(8):
                    n = 8 * c + q
                    out[(128 - n) % 128, pl.ds(row, 16), :] = vals[q]
        return carry

    def two_units(i, carry):
        return unit(2 * i + 1, unit(2 * i, carry))

    lax.fori_loop(0, units // 2, two_units, 0)


def repack(blocks):
    src = in_hbm(jnp.transpose(blocks, (1, 2, 3, 0)))
    ks, width, depth, count = src.shape
    slots = 3
    return pl.pallas_call(
        repack_kernel,
        out_shape=pltpu.VMEM((LANES, ks * depth, 2 * LANES), BF16),
        in_specs=[ASPEC],
        out_specs=VSPEC,
        scratch_shapes=[
            pltpu.VMEM((slots, width, 32, count), BF16),
            pltpu.VMEM((LANES, 16, 2 * LANES), BF16),
            pltpu.SemaphoreType.DMA((slots, 4)),
        ],
        compiler_params=pltpu.CompilerParams(vmem_limit_bytes=16 << 20),
        cost_estimate=pl.CostEstimate(flops=0, bytes_accessed=40 << 20, transcendentals=0),
        name="repack",
    )(src)


def cast_kernel(noise, sent, slab, sems):
    pieces = sems.shape[0]
    width = noise.shape[1] // pieces
    copies = []
    for i in range(pieces):
        cols = slice(i * width, (i + 1) * width)
        copies.append(pltpu.make_async_copy(noise.at[:, cols], slab.at[:, cols], sems.at[i]))
        copies[-1].start()
    for i in range(pieces):
        copies[i].wait()
        cols = slice(i * width, (i + 1) * width)
        sent[:, cols] = slab[:, cols].astype(BF16)


def cast(noise):
    return pl.pallas_call(
        cast_kernel,
        out_shape=(pltpu.VMEM(noise.shape, BF16), pltpu.VMEM(noise.shape, F32)),
        in_specs=[ASPEC],
        out_specs=(VSPEC, VSPEC),
        scratch_shapes=[pltpu.SemaphoreType.DMA((4,))],
        compiler_params=pltpu.CompilerParams(vmem_limit_bytes=4 << 20),
        cost_estimate=pl.CostEstimate(flops=0, bytes_accessed=1 << 20, transcendentals=0),
        name="cast",
    )(in_hbm(noise))


def swap_pair(low, first, second):
    return (
        jnp.where(low, first, pltpu.roll(second, HALF, 1)),
        jnp.where(low, pltpu.roll(first, HALF, 1), second),
    )


def doubled(low, tile):
    turned = pltpu.roll(tile, HALF, 1)
    return [
        jnp.concatenate([t[0:8], t[8:16]], axis=1).astype(BF16)
        for t in (jnp.where(low, tile, turned), jnp.where(low, turned, tile))
    ]


def mix_kernel(noise, following, prev, lag, weights, mixed, half, one, two, ext):
    lags = lag.shape[0]
    steps = noise.shape[0]
    low = lane_bits(2 * steps) < HALF

    def tile(t, slot):
        cols = slice(t * LANES, (t + 1) * LANES)
        ext[slot, 0:8, :] = prev[:, cols].astype(F32)
        ext[slot, 8:16, :] = noise[:, cols]
        ext[slot, 16:24, :] = following[:, cols].astype(F32)
        total = lag[0:1, cols] * ext[slot, 8:24, :]
        for l in range(1, lags):
            total = total + lag[l : l + 1, cols] * ext[slot, 8 - l : 24 - l, :]
        return total

    for g in range(noise.shape[1] // (2 * LANES)):
        h, m = g % 2, g - g % 2
        b, c = block_of(0, h, m), block_of(1, h, m)
        first = tile(b // 2, 2 * g)
        second = tile(c // 2, 2 * g + 1)
        half[b], half[b + 1] = doubled(low, first)
        half[c], half[c + 1] = doubled(low, second)
        mixed[m, h], mixed[m + 1, h] = swap_pair(low, first, second)
    send_edges(masks()[0], half, one, two)


def mix(noise, following, prev, lag, weights):
    rows = 2 * noise.shape[0]
    tiles = noise.shape[1] // LANES
    return pl.pallas_call(
        mix_kernel,
        out_shape=(
            pltpu.VMEM((tiles // 2, 2, rows, LANES), F32),
            pltpu.VMEM((2 * tiles, 8, 2 * LANES), BF16),
            jax.ShapeDtypeStruct((EDGE // 2, 8, 2 * LANES), BF16),
            jax.ShapeDtypeStruct((EDGE // 2, 8, 2 * LANES), BF16),
        ),
        in_specs=[VSPEC] * 5,
        out_specs=(VSPEC,) * 4,
        scratch_shapes=[pltpu.VMEM((tiles, 24, LANES), F32)],
        compiler_params=pltpu.CompilerParams(vmem_limit_bytes=8 << 20),
        cost_estimate=pl.CostEstimate(flops=8 << 20, bytes_accessed=8 << 20, transcendentals=0),
        name="mix",
    )(*[in_vmem(x) for x in (noise, following, prev, lag, weights)])


def halo_block(even, odd, is_odd, at):
    pair = at >> 1
    held = jnp.where(is_odd, odd[pair], even[pair])
    turned = jnp.concatenate(
        [pltpu.roll(held[:, :LANES], HALF, 1), pltpu.roll(held[:, LANES:], HALF, 1)], axis=1
    )
    return jnp.where((at & 1) == 1, held, turned)


def group_product(m, cols, weights, half, low, halos=None):
    halos = halos or {}
    rows = []
    for j in range(4):
        b = block_of(j % 2, j // 2, m)
        picked = []
        for k in range(4):
            c = cols[k, b]
            value = half[c & (PART - 1)]
            if j in halos and k == 1:
                near = (c ^ cols[0, b]) < PART
                value = jnp.where(near, value, halo_block(*halos[j], c & (EDGE - 1)))
            picked.append(value)
        left = jnp.where(low, picked[0], picked[1])
        right = jnp.where(low, picked[2], picked[3])
        rows.append(jnp.concatenate([left[:, :LANES], right[:, :LANES]], axis=1))
        rows.append(jnp.concatenate([left[:, LANES:], right[:, LANES:]], axis=1))
    taken = jnp.concatenate(rows, axis=0)
    y = jnp.dot(taken, weights[m], preferred_element_type=F32)
    turned = ((lane_bits(16) - m) & HALF) == 0
    back = (LANES - m) & (LANES - 1)
    return [
        pltpu.roll(jnp.where(turned, y[r : r + 16, at : at + LANES], y[r + 16 : r + 32, at : at + LANES]), back, 1)
        for r, at in ((0, 0), (32, LANES))
    ]


def masks():
    both = (lax.broadcasted_iota(jnp.int32, (8, 2 * LANES), 1) & HALF) == 0
    return both, lane_bits(16) < HALF


def store_half(half, low, m, pairs):
    for h in range(2):
        half[block_of(0, h, m)], half[block_of(1, h, m)] = doubled(low, pairs[h])


def finish_one(refs, low, m, sums):
    cheb, half = refs
    for h in range(2):
        cheb[m, h] = sums[h]
    store_half(half, low, m, sums)


def finish_two(refs, low, m, sums):
    mixed, cheb, blend, half = refs
    second = []
    for h in range(2):
        at = mixed[m, h]
        second.append(2.0 * sums[h] - at)
        blend[m, h] = 0.75 * at + 0.375 * cheb[m, h] + 0.5 * sums[h]
    store_half(half, low, m, second)


def send_out(buffer, out, sems, units, at):
    copies = []
    for c in range(4):
        start = block_of(c % 2, c // 2, 2 * units[0]) * HALF
        cols = slice(start, start + (units[1] - units[0]) * LANES)
        copies.append(pltpu.make_async_copy(buffer.at[:, cols], out.at[:, cols], sems.at[4 * at + c]))
        copies[-1].start()
    return copies


def finish_three(refs, low, u, filtered):
    lag, out, room, slot = refs
    for h in range(2):
        natural = swap_pair(low, filtered[0][h], filtered[1][h])
        for d in range(2):
            at = slot + 2 * h + d
            room[at] = natural[d]
            cols = pl.ds(pl.multiple_of(block_of(d, h, 2 * u) * HALF, LANES), LANES)
            total = lag[0:1, cols] * natural[d][0:8]
            for l in range(1, lag.shape[0]):
                total = total + lag[l : l + 1, cols] * room[at, l : l + 8, :]
            out[:, cols] = total


EDGE_UNITS = 8
INNER_UNITS = 64 - EDGE_UNITS


def run_inner(body):
    for j in range(INNER_UNITS):
        body(EDGE_UNITS + j, j)


def run_edge(body):
    for j in range(EDGE_UNITS):
        body(j, j)


def pass_call(kernel, cols, weights, half, halos, extra, held, new, edges, scratch, name, space=VSPEC):
    inputs = [weights, half, *halos, *extra]
    aliases = {1 + len(inputs) + i: i for i in range(len(held))} if space is VSPEC else {}
    sent = [jax.ShapeDtypeStruct((EDGE // 2, 8, 2 * LANES), BF16)] * edges
    return pl.pallas_call(
        kernel,
        out_shape=(*new, *sent),
        in_specs=[SSPEC] + [VSPEC] * (len(inputs) + len(held)),
        out_specs=(space,) * len(new) + (VSPEC,) * edges,
        scratch_shapes=scratch,
        input_output_aliases=aliases,
        compiler_params=pltpu.CompilerParams(vmem_limit_bytes=8 << 20),
        cost_estimate=pl.CostEstimate(
            flops=(1 << 26) if held else (1 << 30), bytes_accessed=(1 << 20) if held else (16 << 20), transcendentals=0
        ),
        name=name,
    )(cols, *[in_vmem(x) for x in (*inputs, *held)])


def odd_part():
    return lax.rem(lax.axis_index("mesh"), 2)


def send_edges(both, half, one, two):
    odd = odd_part()
    for to, start in ((one, (1 - odd) * (PART - EDGE)), (two, odd * (PART - EDGE))):
        for i in range(EDGE // 2):
            to[i] = jnp.where(both, half[start + 2 * i], half[start + 2 * i + 1])


def edge_rows(odd, first, second):
    return {0: (second, first, odd), 3: (first, second, odd)}


def inner_one(cols, weights, half, cheb, out_half):
    both, low = masks()

    def body(u, j):
        for d in range(2):
            m = 2 * u + d
            sums = group_product(m, cols, weights, half, both)
            finish_one((cheb, out_half), low, m, sums)

    run_inner(body)


def edge_one(cols, weights, half, first, second, cheb_in, half_in, cheb, out_half, one, two):
    both, low = masks()
    odd = odd_part() == 1

    def body(u, j):
        for d in range(2):
            m = 2 * u + d
            sums = group_product(m, cols, weights, half, both, edge_rows(odd, first, second))
            finish_one((cheb, out_half), low, m, sums)

    run_edge(body)
    send_edges(both, out_half, one, two)


def inner_two(cols, weights, half, mixed, cheb, blend, out_half):
    both, low = masks()

    def body(u, j):
        for d in range(2):
            m = 2 * u + d
            sums = group_product(m, cols, weights, half, both)
            finish_two((mixed, cheb, blend, out_half), low, m, sums)

    run_inner(body)


def edge_two(cols, weights, half, first, second, mixed, cheb, blend_in, half_in, blend, out_half, one, two):
    both, low = masks()
    odd = odd_part() == 1

    def body(u, j):
        for d in range(2):
            m = 2 * u + d
            sums = group_product(m, cols, weights, half, both, edge_rows(odd, first, second))
            finish_two((mixed, cheb, blend, out_half), low, m, sums)

    run_edge(body)
    send_edges(both, out_half, one, two)


def inner_three(cols, weights, half, blend, lag, out, room):
    both, low = masks()

    def body(u, j):
        filtered = []
        for d in range(2):
            m = 2 * u + d
            sums = group_product(m, cols, weights, half, both)
            filtered.append([blend[m, h] + 0.25 * sums[h] for h in range(2)])
        finish_three((lag, out, room, 4 * j), low, u, filtered)

    run_inner(body)


def edge_three(cols, weights, half, first, second, blend, lag, inner, out, room, buffer, sems):
    both, low = masks()
    odd = odd_part() == 1

    copies = send_out(inner, out, sems, (EDGE_UNITS, 64), 0)

    def body(u, j):
        filtered = []
        for d in range(2):
            m = 2 * u + d
            sums = group_product(m, cols, weights, half, both, edge_rows(odd, first, second))
            filtered.append([blend[m, h] + 0.25 * sums[h] for h in range(2)])
        finish_three((lag, buffer, room, 4 * j), low, u, filtered)

    run_edge(body)
    copies += send_out(buffer, out, sems, (0, EDGE_UNITS), 1)
    for copy in copies:
        copy.wait()


def passed_along(value, axis, by):
    peers = lax.axis_size(axis)
    return lax.ppermute(value, axis, [(i, (i + by) % peers) for i in range(peers)])


def edges_passed(one, two):
    parts, slabs = lax.axis_size("mesh"), lax.axis_size("tm")
    near, far = [], []
    for t in range(slabs):
        for p in range(parts):
            for pairs, q in ((near, p ^ 1), (far, ((p + 1) ^ 1) - 1)):
                pairs.append((t * parts + p, t * parts + q if 0 <= q < parts else (t ^ 1) * parts + p))
    return lax.ppermute(one, ("tm", "mesh"), near), lax.ppermute(two, ("tm", "mesh"), far)


def per_device(noise, lag, blocks, block_cols):
    cols = block_cols.T
    sent, slab = cast(noise)
    following = passed_along(sent, "tm", -1)
    prev = passed_along(sent, "tm", 1)
    weights = repack(blocks)
    mixed, half, *sent = mix(slab, following, prev, lag, weights)

    field = pltpu.VMEM(mixed.shape, F32)
    packed = pltpu.VMEM(half.shape, BF16)
    result = pltpu.VMEM(noise.shape, F32)
    inner_room = [pltpu.VMEM((4 * INNER_UNITS, 16, LANES), F32)]
    edge_room = [
        pltpu.VMEM((4 * EDGE_UNITS, 16, LANES), F32),
        pltpu.VMEM(noise.shape, F32),
        pltpu.SemaphoreType.DMA((8,)),
    ]

    halos = edges_passed(*sent)
    held = pass_call(inner_one, cols, weights, half, (), (), (), (field, packed), 0, [], "inner_one")
    cheb, half, *sent = pass_call(
        edge_one, cols, weights, half, halos, (), held, (field, packed), 2, [], "edge_one"
    )
    halos = edges_passed(*sent)
    held = pass_call(inner_two, cols, weights, half, (), (mixed, cheb), (), (field, packed), 0, [], "inner_two")
    blend, half, *sent = pass_call(
        edge_two, cols, weights, half, halos, (mixed, cheb), held, (field, packed), 2, [], "edge_two"
    )
    halos = edges_passed(*sent)
    held = pass_call(inner_three, cols, weights, half, (), (blend, lag), (), (result,), 0, inner_room, "inner_three")
    (out,) = pass_call(
        edge_three, cols, weights, half, halos, (blend, lag), held, (pltpu.HBM(noise.shape, F32),), 0, edge_room, "edge_three", ASPEC
    )
    return out


def solution(mesh):
    placed = (P("tm", "mesh"), P(None, "mesh"), P("mesh", None, None, None), P("mesh", None))
    return jax.shard_map(
        per_device, mesh=mesh, in_specs=placed, out_specs=P("tm", "mesh"), check_vma=False
    )
```
